512 devices in a mesh: space: 32 (over z, core), mode: 16 (over y, x).
Axes of the slice: x: 4, y: 4, z: 16, core: 2. Of those that a mesh axis runs over, the one named last changes fastest.
Arguments:
- basis: float32 [65536, 1024], P('space', 'mode'), may hold values from -0.0234375 to 0.0234375
- snapshots: float32 [65536, 64], P('space'), may hold values from -6 to 6
- rotation: float32 [1088, 1024], replicated, may hold values from -0.1875 to 0.1875
Outputs:
- scaled_basis: float32 [65536, 1024], P('space', 'mode')
- factor: float32 [64, 64], replicated
The draws below stay inside these ranges and needn't reach their ends.
All inputs are finite; a program needn't handle non-finite values.
Results may differ from the reference program's by a relative error of at most 0.00007.
Values sent between devices are 32-bit elements; how exact they have to be, the bound alone decides.
No kernel may reach another device: no remote copies, remote signals or barrier semaphores. Data moves between devices by JAX's collectives and lax.ppermute only.
A program may use at most 64 MiB of HBM per device.

```python
import jax
import jax.numpy as jnp
from jax import lax

K = 1024
P_SIZE = 64
ROWS = 65536


def steps_of(rng, dims, split, low, largest):
    def one(dim, parts):
        steps = jax.random.uniform(jax.random.fold_in(jax.random.fold_in(rng, 6), dim), (parts,), jnp.float32, low / len(split), largest / len(split))
        return jnp.repeat(jnp.exp(steps), dims[dim] // parts).reshape((-1,) + (1,) * (len(dims) - dim - 1))

    factor_of = one(*split[0])
    for cut in split[1:]:
        factor_of = factor_of * one(*cut)
    return factor_of


def noise(key, extent, width, limit, split=(), held_as=jnp.bfloat16):
    result = width * jax.random.normal(key, extent, jnp.float32)
    if split:
        result = result * steps_of(key, extent, split, -0.22, 0.18)
    return jnp.clip(result, -limit, limit).astype(held_as)


def setup_inputs(seed: int = 0) -> dict:
    keys = jax.random.split(jax.random.key(seed), 4)
    return {
        "basis": noise(keys[0], (ROWS, K), ROWS ** -0.5, 0.0234375, ((0, 32), (1, 16)), jnp.float32),
        "snapshots": noise(keys[1], (ROWS, P_SIZE), 1.0, 6.0, ((0, 32),), jnp.float32),
        "rotation": noise(keys[2], (K + P_SIZE, K), (K + P_SIZE) ** -0.5, 0.1875, (), jnp.float32),
    }


def reference(basis, snapshots, rotation):
    high = lax.Precision.HIGHEST
    coeffs = jnp.dot(basis.T, snapshots, precision=high)
    resid = snapshots - jnp.dot(basis, coeffs, precision=high)
    gram = jnp.dot(resid.T, resid, precision=high)
    lower = jnp.linalg.cholesky(gram)
    ortho = lax.linalg.triangular_solve(lower, resid, left_side=False, lower=True, transpose_a=True)
    updated = jnp.dot(basis, rotation[:K], precision=high) + jnp.dot(ortho, rotation[K:], precision=high)
    scale = jnp.sqrt(jnp.float32(ROWS))
    return (updated * scale, lower / scale)
```

```python
import jax
import jax.numpy as jnp
from jax import lax
from jax.sharding import Mesh, PartitionSpec as P

HIGH = lax.Precision.HIGHEST
Z = "z"
CORE = "core"
MODE = ("y", "x")


def spread(block, axes, count):
    return lax.all_to_all(
        jnp.broadcast_to(block[None], (count,) + block.shape), axes, 0, 0, tiled=True
    )


def dot(a, b, left, right):
    return lax.dot_general(a, b, (((left,), (right,)), ((), ())), precision=HIGH)


def local(basis, snapshots, rotation):
    depth = lax.axis_size(Z)
    modes = lax.axis_size("y") * lax.axis_size("x")
    rows, width = basis.shape
    count = snapshots.shape[1]
    part = rows // modes
    total = rotation.shape[1]
    place = lax.axis_index(MODE)
    scale = jnp.sqrt(jnp.float32(rows * depth * 2))
    bt, st = basis.T, snapshots.T
    own = lax.all_to_all(bt.reshape(width, modes, part), MODE, 1, 0, tiled=False)
    own = own.reshape(total, part)
    coeffs = dot(bt, st, 1, 1)
    half = lax.all_to_all(coeffs.reshape(2, width // 2, count), CORE, 0, 0, tiled=True)
    half = spread(half.sum(0), Z, depth).sum(0)
    coeffs_all = spread(half, MODE + (CORE,), modes * 2).reshape(total, count)
    st_own = lax.dynamic_slice_in_dim(st, place * part, part, 1)
    resid = st_own - dot(coeffs_all, own, 0, 0)
    gram = dot(resid, resid, 1, 1)
    pieces = jnp.broadcast_to(
        gram.reshape(2, 1, count // 2, count), (2, modes, count // 2, count)
    ).reshape(2 * modes, count // 2, count)
    pieces = lax.all_to_all(pieces, (CORE,) + MODE, 0, 0, tiled=True).sum(0)
    pieces = spread(pieces, Z, depth).sum(0)
    gram = lax.all_gather(pieces, CORE, axis=0, tiled=True)
    lower = jnp.linalg.cholesky(gram)
    columns = lax.dynamic_slice_in_dim(rotation, place * width, width, 1)
    weights = lax.linalg.triangular_solve(
        lower, columns[total:], left_side=True, lower=True, transpose_a=True
    )
    rotated = dot(rotation[:total], own, 0, 0)
    rotated = lax.all_to_all(rotated.reshape(modes, width, part), MODE, 0, 1, tiled=False)
    rotated = rotated.reshape(width, rows)
    resid_all = lax.all_to_all(
        jnp.broadcast_to(resid[None], (modes, count, part)), MODE, 0, 1, tiled=False
    ).reshape(count, rows)
    updated = rotated + dot(weights, resid_all, 0, 0)
    return ((updated * scale).T, lower / scale)


def solution(mesh):
    y, x = 4, 4
    split = Mesh(mesh.devices.reshape(-1, 2, y, x), ("z", "core", "y", "x"))
    space, mode = ("z", "core"), ("y", "x")
    placed = (P(space, mode), P(space, None), P())
    return jax.shard_map(
        local, mesh=split, in_specs=placed, out_specs=(P(space, mode), P()), check_vma=False
    )
```

```python
import functools

import jax
import jax.numpy as jnp
from jax import lax
from jax.experimental import pallas as pl
from jax.experimental.pallas import tpu as pltpu
from jax.sharding import Mesh, PartitionSpec as P

HIGH = lax.Precision.HIGH
Z = "z"
CORE = "core"
MODE = ("y", "x")


def spread(block, axes, count):
    return lax.all_to_all(
        jnp.broadcast_to(block[None], (count,) + block.shape), axes, 0, 0, tiled=True
    )


def dot(a, b, left, right):
    return lax.dot_general(a, b, (((left,), (right,)), ((), ())), precision=HIGH)


def pack(block):
    half = block.shape[0] // 2
    return jnp.concatenate([block[:half], block[half:]], 1)


def unpack(block):
    half = block.shape[1] // 2
    return jnp.concatenate([block[:, :half], block[:, half:]], 0)


def over_space(block, depth):
    both = lax.all_gather(block, CORE, axis=0, tiled=False).sum(0)
    half = both.shape[0] // 2
    mine = lax.dynamic_slice_in_dim(both, lax.axis_index(CORE) * half, half, 0)
    mine = spread(mine, Z, depth).sum(0)
    return lax.all_gather(mine, CORE, axis=0, tiled=True)


def halves(a):
    top = a.astype(jnp.bfloat16)
    return top, (a - top.astype(jnp.float32)).astype(jnp.bfloat16)


def dot3(a, b, dims=((1,), (0,))):
    (ah, al), (bh, bl) = halves(a), halves(b)
    one = lambda p, q: lax.dot_general(p, q, (dims, ((), ())), preferred_element_type=jnp.float32)
    return one(ah, bh) + (one(ah, bl) + one(al, bh))


def finish(scale, gram_ref, lower_cols_ref, parts_ref, out_ref, factor_ref):
    count = lower_cols_ref.shape[0]
    tiles = count // 8
    packed = gram_ref[...]
    lane = lax.broadcasted_iota(jnp.int32, (8, 2 * count), 1)
    sub = lax.broadcasted_iota(jnp.int32, (8, 2 * count), 0)
    gram = jnp.concatenate([packed[:, :count], packed[:, count:]], 0)
    wide = jnp.concatenate([gram, jnp.zeros((count, count), jnp.float32)], 1)
    rows = [
        jnp.where(lane == sub + (8 * t + count), 1.0, wide[8 * t : 8 * t + 8])
        for t in range(tiles)
    ]
    for j in range(count):
        b, r = divmod(j, 8)
        column = [jnp.broadcast_to(rows[t][:, j : j + 1], (8, 2 * count)) for t in range(b, tiles)]
        pivot = jnp.broadcast_to(column[0][r : r + 1], (8, 2 * count))
        scaled = jnp.broadcast_to(rows[b][r : r + 1], (8, 2 * count)) / pivot
        rows[b] = rows[b] - jnp.where(sub > r, column[0], 0.0) * scaled
        for t in range(b + 1, tiles):
            rows[t] = rows[t] - column[t - b] * scaled
    done = []
    for t in range(tiles):
        diag = jnp.sum(jnp.where(lane == sub + 8 * t, rows[t], 0.0), 1, keepdims=True)
        done.append(jnp.where(lane >= sub + 8 * t, rows[t] * lax.rsqrt(diag), 0.0))
    done = jnp.concatenate(done, 0)
    factor_ref[...] = done[:, :count].T * (1.0 / scale)
    weights = dot3(lower_cols_ref[...].T, done[:, count:]) * scale
    part = parts_ref.shape[2]
    for j in range(parts_ref.shape[0]):
        piece = parts_ref[j]
        out_ref[:, j * part : (j + 1) * part] = piece[:count] * scale + dot3(
            weights, piece[count : 2 * count]
        )


def local(basis, snapshots, rotation):
    depth = lax.axis_size(Z)
    modes = lax.axis_size("y") * lax.axis_size("x")
    rows, width = basis.shape
    count = snapshots.shape[1]
    part = rows // modes
    total = rotation.shape[1]
    place = lax.axis_index(MODE)
    scale = float(rows * depth * 2) ** 0.5
    bt, st = basis.T, snapshots.T
    tiles = bt.reshape(width, modes, part).transpose(1, 0, 2)
    coeffs = over_space(pack(dot(bt, st, 1, 1)), depth)
    coeffs = jnp.broadcast_to(coeffs[None], (modes,) + coeffs.shape)
    got = lax.all_to_all(jnp.concatenate([tiles, coeffs], 1), MODE, 0, 0, tiled=True)
    own = got[:, :width].reshape(total, part)
    coeffs = got[:, width:]
    coeffs = jnp.concatenate([coeffs[:, :, :count], coeffs[:, :, count:]], 1).reshape(total, count)
    resid = lax.dynamic_slice_in_dim(st, place * part, part, 1) - dot(coeffs, own, 0, 0)
    gram = dot(resid, resid, 1, 1)
    rotated = dot(rotation[:total], own, 0, 0).reshape(modes, width, part)
    rest = jnp.concatenate([resid, pack(gram)], 0)
    rest = jnp.broadcast_to(rest[None], (modes,) + rest.shape)
    parts = lax.all_to_all(jnp.concatenate([rotated, rest], 1), MODE, 0, 0, tiled=True)
    gram = over_space(parts[:, width + count :].sum(0), depth)
    lower_cols = lax.dynamic_slice(rotation, (total, place * width), (count, width))
    vmem = pl.BlockSpec(memory_space=pltpu.VMEM)
    out, factor = pl.pallas_call(
        functools.partial(finish, scale),
        out_shape=(
            jax.ShapeDtypeStruct((width, rows), jnp.float32),
            jax.ShapeDtypeStruct((count, count), jnp.float32),
        ),
        in_specs=[vmem] * 3,
        out_specs=(vmem, vmem),
        compiler_params=pltpu.CompilerParams(vmem_limit_bytes=32 << 20),
        name="finish",
    )(gram, lower_cols, parts)
    return out.T, factor


def solution(mesh):
    y, x = 4, 4
    split = Mesh(mesh.devices.reshape(-1, 2, y, x), ("z", "core", "y", "x"))
    space, mode = ("z", "core"), ("y", "x")
    placed = (P(space, mode), P(space, None), P())
    return jax.shard_map(
        local, mesh=split, in_specs=placed, out_specs=(P(space, mode), P()), check_vma=False
    )
```

```python
import functools

import jax
import jax.numpy as jnp
from jax import lax
from jax.experimental import pallas as pl
from jax.experimental.pallas import tpu as pltpu
from jax.sharding import Mesh, PartitionSpec as P

HIGH = lax.Precision.HIGH
Z = "z"
CORE = "core"
MODE = ("y", "x")
STEP = 8
CHUNKS = 4
VMEM = pl.BlockSpec(memory_space=pltpu.VMEM)
ANY = pl.BlockSpec(memory_space=pl.ANY)
LIMIT = pltpu.CompilerParams(vmem_limit_bytes=32 << 20)


def struct(*shape):
    return jax.ShapeDtypeStruct(shape, jnp.float32)


def spread(block, axes, count):
    return lax.all_to_all(
        jnp.broadcast_to(block[None], (count,) + block.shape), axes, 0, 0, tiled=True
    )


def dot(a, b, left, right):
    return lax.dot_general(a, b, (((left,), (right,)), ((), ())), precision=HIGH)


def halves(a):
    top = a.astype(jnp.bfloat16)
    return top, (a - top.astype(jnp.float32)).astype(jnp.bfloat16)


def dot3(a, b, left=1, right=0):
    (ah, al), (bh, bl) = halves(a), halves(b)

    def one(p, q):
        dims = (((left,), (right,)), ((), ()))
        return lax.dot_general(p, q, dims, preferred_element_type=jnp.float32)

    return one(ah, bh) + (one(ah, bl) + one(al, bh))


def pack(block):
    half = block.shape[0] // 2
    return jnp.concatenate([block[:half], block[half:]], 1)


def project(bt_ref, st_ref, out_ref, b_buf, s_buf, sems):
    step = b_buf.shape[1] // CHUNKS
    copies = []
    for i in range(CHUNKS):
        cut = pl.ds(i * step, step)
        for k, (src, dst) in enumerate(((bt_ref, b_buf), (st_ref, s_buf))):
            copy = pltpu.make_async_copy(src.at[:, cut], dst.at[:, cut], sems.at[2 * i + k])
            copy.start()
            copies.append(copy)
    total = None
    for i in range(CHUNKS):
        copies[2 * i].wait()
        copies[2 * i + 1].wait()
        cut = slice(i * step, (i + 1) * step)
        term = dot3(b_buf[:, cut], s_buf[:, cut], 1, 1)
        total = term if total is None else total + term
    out_ref[...] = pack(total)


def remainder(got_ref, st_ref, resid_ref, gram_ref):
    modes, _, part = got_ref.shape
    count = st_ref.shape[0]
    width = got_ref.shape[1] - count // 2
    half = width // 2
    got = got_ref[...]
    upper = got[:, :half].reshape(modes * half, part)
    lower = got[:, half:width].reshape(modes * half, part)
    coeffs = got[:, width:].reshape(modes * half, 2 * count)
    both = dot3(coeffs.T, jnp.concatenate([upper, lower], 1))
    resid = st_ref[...] - (both[:count, :part] + both[count:, part:])
    resid_ref[...] = resid
    gram_ref[...] = pack(dot3(resid, resid, 1, 1))


def eliminate(gram):
    count = gram.shape[0]
    tiles = count // STEP
    shape = (STEP, 2 * count)
    lane = lax.broadcasted_iota(jnp.int32, shape, 1)
    sub = lax.broadcasted_iota(jnp.int32, shape, 0)
    wide = jnp.concatenate([gram, jnp.zeros((count, count), jnp.float32)], 1)
    rows = [
        jnp.where(lane == sub + (STEP * t + count), 1.0, wide[STEP * t : STEP * (t + 1)])
        for t in range(tiles)
    ]
    done = []
    for b in range(tiles):
        later = range(b + 1, tiles)
        first = STEP * b
        block = [
            jnp.broadcast_to(rows[b][:, first + k : first + k + 1], shape) for k in range(STEP)
        ]
        column = [
            {t: jnp.broadcast_to(rows[t][:, first + k : first + k + 1], shape) for t in later}
            for k in range(STEP)
        ]
        row = [jnp.broadcast_to(rows[b][k : k + 1], shape) for k in range(STEP)]
        pivot = {
            (i, k): jnp.broadcast_to(block[k][i : i + 1], shape)
            for i in range(STEP)
            for k in range(i + 1)
        }
        scaled = []
        for k in range(STEP):
            inverse = 1.0 / pivot[k, k]
            scaled.append(row[k] * inverse)
            for i in range(k + 1, STEP):
                ratio = pivot[i, k] * inverse
                for m in range(k + 1, i + 1):
                    pivot[i, m] = pivot[i, m] - ratio * pivot[m, k]
                row[i] = row[i] - ratio * row[k]
                for t in later:
                    column[i][t] = column[i][t] - ratio * column[k][t]
        for t in later:
            for k in range(STEP):
                rows[t] = rows[t] - column[k][t] * scaled[k]
        final = jnp.zeros(shape, jnp.float32)
        for k in range(STEP):
            final = jnp.where(sub == k, row[k] * lax.rsqrt(pivot[k, k]), final)
        done.append(jnp.where(lane >= sub + first, final, 0.0))
    return jnp.concatenate(done, 0)


def finish(scale, gram_ref, lower_cols_ref, parts_ref, out_ref, factor_ref):
    count = lower_cols_ref.shape[0]
    packed = gram_ref[...]
    done = eliminate(jnp.concatenate([packed[:, :count], packed[:, count:]], 0))
    factor_ref[...] = done[:, :count].T * (1.0 / scale)
    weights = dot3(lower_cols_ref[...].T, done[:, count:]) * scale
    modes, _, part = parts_ref.shape
    for j in range(modes):
        piece = parts_ref[j]
        out_ref[:, j * part : (j + 1) * part] = piece[:count] * scale + dot3(
            weights, piece[count : 2 * count]
        )


def core_half(block):
    both = lax.all_gather(block, CORE, axis=0, tiled=False).sum(0)
    half = both.shape[0] // 2
    return lax.dynamic_slice_in_dim(both, lax.axis_index(CORE) * half, half, 0)


def local(basis, snapshots, rotation):
    depth = lax.axis_size(Z)
    modes = lax.axis_size("y") * lax.axis_size("x")
    rows, width = basis.shape
    count = snapshots.shape[1]
    part = rows // modes
    total = rotation.shape[1]
    place = lax.axis_index(MODE)
    scale = float(rows * depth * 2) ** 0.5
    bt, st = basis.T, snapshots.T
    coeffs = pl.pallas_call(
        project,
        out_shape=struct(width // 2, 2 * count),
        in_specs=[ANY, ANY],
        out_specs=VMEM,
        scratch_shapes=[
            pltpu.VMEM((width, rows), jnp.float32),
            pltpu.VMEM((count, rows), jnp.float32),
            pltpu.SemaphoreType.DMA((2 * CHUNKS,)),
        ],
        compiler_params=LIMIT,
        name="project",
    )(bt, st)
    coeffs = spread(core_half(coeffs), Z, depth).sum(0)
    coeffs = lax.all_gather(coeffs, CORE, axis=0, tiled=True)
    pieces = bt.reshape(width, modes, part).transpose(1, 0, 2)
    pieces = jnp.concatenate([pieces, jnp.zeros((modes, width // 2, part), jnp.float32)], 1)
    pieces = lax.dynamic_update_slice(
        pieces, jnp.broadcast_to(coeffs[None], (modes,) + coeffs.shape), (0, width, 0)
    )
    got = lax.all_to_all(pieces, MODE, 0, 0, tiled=True)
    resid, gram = pl.pallas_call(
        remainder,
        out_shape=(struct(count, part), struct(count // 2, 2 * count)),
        in_specs=[VMEM, VMEM],
        out_specs=(VMEM, VMEM),
        compiler_params=LIMIT,
        name="remainder",
    )(got, lax.dynamic_slice_in_dim(st, place * part, part, 1))
    gram = spread(core_half(gram), Z, depth).sum(0)
    own = got[:, :width].reshape(total, part)
    rotated = dot(rotation[:total], own, 0, 0).reshape(modes, width, part)
    resid = jnp.broadcast_to(resid[None], (modes,) + resid.shape)
    empty = jnp.zeros((modes,) + gram.shape, jnp.float32)
    pieces = lax.dynamic_update_slice(
        jnp.concatenate([rotated, resid, empty], 1),
        jnp.broadcast_to(gram[None], (modes,) + gram.shape),
        (0, width + count, 0),
    )
    parts = lax.all_to_all(pieces, MODE, 0, 0, tiled=True)
    gram = lax.all_gather(parts[:, width + count :].sum(0), CORE, axis=0, tiled=True)
    lower_cols = lax.dynamic_slice(rotation, (total, place * width), (count, width))
    out, factor = pl.pallas_call(
        functools.partial(finish, scale),
        out_shape=(struct(width, rows), struct(count, count)),
        in_specs=[VMEM] * 3,
        out_specs=(VMEM, VMEM),
        compiler_params=LIMIT,
        name="finish",
    )(gram, lower_cols, parts)
    return out.T, factor


def solution(mesh):
    y, x = 4, 4
    split = Mesh(mesh.devices.reshape(-1, 2, y, x), ("z", "core", "y", "x"))
    space, mode = ("z", "core"), ("y", "x")
    placed = (P(space, mode), P(space, None), P())
    return jax.shard_map(
        local, mesh=split, in_specs=placed, out_specs=(P(space, mode), P()), check_vma=False
    )
```

```python
import functools

import jax
import jax.numpy as jnp
from jax import lax
from jax.experimental import pallas as pl
from jax.experimental.pallas import tpu as pltpu
from jax.sharding import Mesh, PartitionSpec as P

HIGH = lax.Precision.HIGH
Z = "z"
CORE = "core"
MODE = ("y", "x")
STEP = 8
CHUNKS = 4
VMEM = pl.BlockSpec(memory_space=pltpu.VMEM)
HBM = pl.BlockSpec(memory_space=pltpu.HBM)
FULL = pltpu.CompilerParams(vmem_limit_bytes=55_800_000)
LIMIT = pltpu.CompilerParams(vmem_limit_bytes=32 << 20)


def struct(*shape):
    return jax.ShapeDtypeStruct(shape, jnp.float32)


def spread(block, axes, count):
    return lax.all_to_all(
        jnp.broadcast_to(block[None], (count,) + block.shape), axes, 0, 0, tiled=True
    )


def dot(a, b, left, right):
    return lax.dot_general(a, b, (((left,), (right,)), ((), ())), precision=HIGH)


def halves(a):
    top = a.astype(jnp.bfloat16)
    return top, (a - top.astype(jnp.float32)).astype(jnp.bfloat16)


def dot3(a, b, left=1, right=0):
    (ah, al), (bh, bl) = halves(a), halves(b)

    def one(p, q):
        dims = (((left,), (right,)), ((), ()))
        return lax.dot_general(p, q, dims, preferred_element_type=jnp.float32)

    return one(ah, bh) + (one(ah, bl) + one(al, bh))


def pack(block):
    half = block.shape[0] // 2
    return jnp.concatenate([block[:half], block[half:]], 1)


def project(bt_ref, st_ref, coeffs_ref, pieces_ref, own_ref, b_buf, s_buf, sems):
    step = b_buf.shape[1] // CHUNKS
    copies = []
    for i in range(CHUNKS):
        cut = pl.ds(i * step, step)
        for k, (src, dst) in enumerate(((bt_ref, b_buf), (st_ref, s_buf))):
            copy = pltpu.make_async_copy(src.at[:, cut], dst.at[:, cut], sems.at[2 * i + k])
            copy.start()
            copies.append(copy)
    part = pieces_ref.shape[2]
    each = step // part
    total = None
    for i in range(CHUNKS):
        copies[2 * i].wait()
        copies[2 * i + 1].wait()
        cut = slice(i * step, (i + 1) * step)
        basis = b_buf[:, cut]
        term = dot3(basis, s_buf[:, cut], 1, 1)
        total = term if total is None else total + term
        for j in range(each):
            pieces_ref[i * each + j] = basis[:, j * part : (j + 1) * part]
    coeffs_ref[...] = pack(total)
    place = lax.axis_index("y") * lax.axis_size("x") + lax.axis_index("x")
    own_ref[...] = s_buf[:, pl.ds(pl.multiple_of(place * part, part), part)]


def share(both_ref, out_ref):
    half = out_ref.shape[1]
    both = both_ref[0] + both_ref[1]
    mine = jnp.where(lax.axis_index(CORE) == 0, both[:half], both[half:])
    for k in range(out_ref.shape[0]):
        out_ref[k] = mine


def added(ref):
    total = ref[0]
    for k in range(1, ref.shape[0]):
        total = total + ref[k]
    return total


def bundle(coeffs_ref, pieces_ref, out_ref):
    width = pieces_ref.shape[1]
    out_ref[:, :width] = pieces_ref[...]
    coeffs = added(coeffs_ref)
    for j in range(out_ref.shape[0]):
        out_ref[j, width:] = coeffs


def bundle_back(gram_ref, rotated_ref, resid_ref, cols_ref, out_ref, cols_out_ref):
    width, count = rotated_ref.shape[1], resid_ref.shape[0]
    out_ref[:, :width] = rotated_ref[...]
    gram, resid = added(gram_ref), resid_ref[...]
    for j in range(out_ref.shape[0]):
        out_ref[j, width : width + count] = resid
        out_ref[j, width + count :] = gram
    cols_out_ref[...] = cols_ref[...]


def remainder(got_ref, coeffs_ref, st_ref, resid_ref, gram_ref):
    modes, _, part = got_ref.shape
    cores, _, few, _ = coeffs_ref.shape
    count = st_ref.shape[0]

    def stack(first):
        cuts = [got_ref[:, first + c * few : first + (c + 1) * few] for c in range(cores)]
        return jnp.concatenate([cut.reshape(modes * few, part) for cut in cuts], 0)

    coeffs = coeffs_ref[...].reshape(cores * modes * few, 2 * count)
    both = dot3(coeffs.T, jnp.concatenate([stack(0), stack(cores * few)], 1))
    resid = st_ref[...] - (both[:count, :part] + both[count:, part:])
    resid_ref[...] = resid
    gram_ref[...] = pack(dot3(resid, resid, 1, 1))


def eliminate(gram):
    count = gram.shape[0]
    tiles = count // STEP
    shape = (STEP, 2 * count)
    lane = lax.broadcasted_iota(jnp.int32, shape, 1)
    sub = lax.broadcasted_iota(jnp.int32, shape, 0)
    wide = jnp.concatenate([gram, jnp.zeros((count, count), jnp.float32)], 1)
    rows = [
        jnp.where(lane == sub + (STEP * t + count), 1.0, wide[STEP * t : STEP * (t + 1)])
        for t in range(tiles)
    ]
    done = []
    for b in range(tiles):
        later = range(b + 1, tiles)
        first = STEP * b
        block = [
            jnp.broadcast_to(rows[b][:, first + k : first + k + 1], shape) for k in range(STEP)
        ]
        column = [
            {t: jnp.broadcast_to(rows[t][:, first + k : first + k + 1], shape) for t in later}
            for k in range(STEP)
        ]
        row = [jnp.broadcast_to(rows[b][k : k + 1], shape) for k in range(STEP)]
        pivot = {
            (i, k): jnp.broadcast_to(block[k][i : i + 1], shape)
            for i in range(STEP)
            for k in range(i + 1)
        }
        scaled = []
        for k in range(STEP):
            inverse = 1.0 / pivot[k, k]
            scaled.append(row[k] * inverse)
            for i in range(k + 1, STEP):
                ratio = pivot[i, k] * inverse
                for m in range(k + 1, i + 1):
                    pivot[i, m] = pivot[i, m] - ratio * pivot[m, k]
                row[i] = row[i] - ratio * row[k]
                for t in later:
                    column[i][t] = column[i][t] - ratio * column[k][t]
        for t in later:
            for k in range(STEP):
                rows[t] = rows[t] - column[k][t] * scaled[k]
        final = jnp.zeros(shape, jnp.float32)
        for k in range(STEP):
            final = jnp.where(sub == k, row[k] * lax.rsqrt(pivot[k, k]), final)
        done.append(jnp.where(lane >= sub + first, final, 0.0))
    return jnp.concatenate(done, 0)


def finish(scale, gram_ref, lower_cols_ref, parts_ref, out_ref, factor_ref):
    count = lower_cols_ref.shape[0]
    packed = gram_ref[...]
    done = eliminate(jnp.concatenate([packed[:, :count], packed[:, count:]], 0))
    factor_ref[...] = done[:, :count].T * (1.0 / scale)
    weights = dot3(lower_cols_ref[...].T, done[:, count:]) * scale
    modes, _, part = parts_ref.shape
    for j in range(modes):
        piece = parts_ref[j]
        out_ref[:, j * part : (j + 1) * part] = piece[:count] * scale + dot3(
            weights, piece[count : 2 * count]
        )


def kernel(body, out, args, specs=None, scratch=(), params=LIMIT):
    return pl.pallas_call(
        body,
        out_shape=out,
        in_specs=specs or [VMEM] * len(args),
        out_specs=(VMEM,) * len(out) if isinstance(out, tuple) else VMEM,
        scratch_shapes=scratch,
        compiler_params=params,
    )(*args)


def over_space(block, depth):
    both = lax.all_gather(block, CORE, axis=0, tiled=False)
    few = block.shape[0] // 2
    return lax.all_to_all(
        kernel(share, struct(depth, few, block.shape[1]), (both,)), Z, 0, 0, tiled=True
    )


def local(basis, snapshots, rotation):
    depth = lax.axis_size(Z)
    modes = lax.axis_size("y") * lax.axis_size("x")
    rows, width = basis.shape
    count = snapshots.shape[1]
    part = rows // modes
    few = width // 4
    total = rotation.shape[1]
    place = lax.axis_index(MODE)
    scale = float(rows * depth * 2) ** 0.5
    bt, st = basis.T, snapshots.T
    buffers = (
        pltpu.VMEM((width, rows), jnp.float32),
        pltpu.VMEM((count, rows), jnp.float32),
        pltpu.SemaphoreType.DMA((2 * CHUNKS,)),
    )
    coeffs, pieces, st_own = kernel(
        project,
        (struct(width // 2, 2 * count), struct(modes, width, part), struct(count, part)),
        (bt, st),
        [HBM, HBM],
        buffers,
        FULL,
    )
    coeffs = over_space(coeffs, depth)
    got = kernel(bundle, struct(modes, width + few, part), (coeffs, pieces))
    got = lax.all_to_all(got, MODE, 0, 0, tiled=True)
    coeffs = lax.all_gather(got[:, width:], CORE, axis=0, tiled=False)
    resid, gram = kernel(
        remainder,
        (struct(count, part), struct(count // 2, 2 * count)),
        (got, coeffs, st_own),
    )
    gram = over_space(gram, depth)
    own = got[:, :width].reshape(total, part)
    rotated = dot(rotation[:total], own, 0, 0).reshape(modes, width, part)
    lower_cols = lax.dynamic_slice(rotation, (total, place * width), (count, width))
    pieces, lower_cols = kernel(
        bundle_back,
        (struct(modes, width + count + few, part), struct(count, width)),
        (gram, rotated, resid, lower_cols),
    )
    parts = lax.all_to_all(pieces, MODE, 0, 0, tiled=True)
    gram = lax.all_gather(parts[:, width + count :].sum(0), CORE, axis=0, tiled=True)
    out, factor = kernel(
        functools.partial(finish, scale),
        (struct(width, rows), struct(count, count)),
        (gram, lower_cols, parts),
    )
    return out.T, factor


def solution(mesh):
    y, x = 4, 4
    split = Mesh(mesh.devices.reshape(-1, 2, y, x), ("z", "core", "y", "x"))
    space, mode = ("z", "core"), ("y", "x")
    placed = (P(space, mode), P(space, None), P())
    return jax.shard_map(
        local, mesh=split, in_specs=placed, out_specs=(P(space, mode), P()), check_vma=False
    )
```

```python
import functools

import jax
import jax.numpy as jnp
import numpy as np
from jax import lax
from jax.experimental import pallas as pl
from jax.experimental.pallas import tpu as pltpu
from jax.sharding import Mesh, PartitionSpec as P

HIGH = lax.Precision.HIGH
Z = "z"
CORE = "core"
MODE = ("y", "x")
STEP = 8
CHUNKS = 4
VMEM = pl.BlockSpec(memory_space=pltpu.VMEM)
HBM = pl.BlockSpec(memory_space=pltpu.HBM)
FULL = pltpu.CompilerParams(vmem_limit_bytes=55_800_000)
LIMIT = pltpu.CompilerParams(vmem_limit_bytes=32 << 20)


def struct(*shape):
    return jax.ShapeDtypeStruct(shape, jnp.float32)


def dot(a, b, left, right):
    return lax.dot_general(a, b, (((left,), (right,)), ((), ())), precision=HIGH)


def halves(a):
    top = a.astype(jnp.bfloat16)
    return top, (a - top.astype(jnp.float32)).astype(jnp.bfloat16)


def dot3(a, b, left=1, right=0):
    (ah, al), (bh, bl) = halves(a), halves(b)

    def one(p, q):
        dims = (((left,), (right,)), ((), ()))
        return lax.dot_general(p, q, dims, preferred_element_type=jnp.float32)

    return one(ah, bh) + (one(ah, bl) + one(al, bh))


def pack(block):
    half = block.shape[0] // 2
    return jnp.concatenate([block[:half], block[half:]], 1)


def project(bt_ref, st_ref, first_ref, pieces_ref, own_ref, b_buf, s_buf, sems):
    step = b_buf.shape[1] // CHUNKS
    copies = []
    for i in range(CHUNKS):
        cut = pl.ds(i * step, step)
        for k, (src, dst) in enumerate(((bt_ref, b_buf), (st_ref, s_buf))):
            copy = pltpu.make_async_copy(src.at[:, cut], dst.at[:, cut], sems.at[2 * i + k])
            copy.start()
            copies.append(copy)
    _, width, part = pieces_ref.shape
    each, half = step // part, width // 2
    total = None
    for i in range(CHUNKS):
        copies[2 * i].wait()
        copies[2 * i + 1].wait()
        cut = slice(i * step, (i + 1) * step)
        basis = b_buf[:, cut]
        term = dot3(basis, s_buf[:, cut], 1, 1)
        total = term if total is None else total + term
        for j in range(i * each, (i + 1) * each):
            piece = b_buf[:, j * part : (j + 1) * part]
            pieces_ref[j] = piece
            first_ref[(j + 1) * half : (j + 2) * half] = piece[half:]
    first_ref[:half] = pack(total)
    place = lax.axis_index("y") * lax.axis_size("x") + lax.axis_index("x")
    own_ref[...] = s_buf[:, pl.ds(pl.multiple_of(place * part, part), part)]


def first_core():
    return lax.axis_index(CORE) == 0


def share(both_ref, out_ref):
    count, half, _ = out_ref.shape
    coeffs = both_ref[0, :half] + both_ref[1, :half]
    for k in range(count):
        piece = both_ref[1, (k + 1) * half : (k + 2) * half]
        out_ref[k] = jnp.where(first_core(), piece, coeffs)


def share_back(both_ref, out_ref):
    half = out_ref.shape[1]
    gram = both_ref[0, :half] + both_ref[1, :half]
    mine = jnp.where(first_core(), both_ref[1, half:], gram)
    for k in range(out_ref.shape[0]):
        out_ref[k] = mine


def added(ref):
    total = ref[0]
    for k in range(1, ref.shape[0]):
        total = total + ref[k]
    return total


def bundle(crossed_ref, pieces_ref, out_ref):
    half = crossed_ref.shape[1]
    coeffs = added(crossed_ref)
    out_ref[:, :half] = pieces_ref[:, :half]
    for j in range(out_ref.shape[0]):
        out_ref[j, half:] = jnp.where(first_core(), pieces_ref[j, half:], coeffs)


def trade(crossed_ref, got_ref, out_ref):
    half = crossed_ref.shape[1]
    out_ref[...] = jnp.where(first_core(), crossed_ref[...], got_ref[:, half:])


def remainder(got_ref, traded_ref, st_ref, resid_ref, both_ref):
    modes, width, part = got_ref.shape
    count = st_ref.shape[0]
    half = width // 2
    lower = got_ref[:, :half]
    upper = jnp.where(first_core(), got_ref[:, half:], traded_ref[0])
    rows = [block.reshape(modes * half, part) for block in (lower, upper)]
    coeffs = traded_ref[1].reshape(modes * half, 2 * count)
    back = dot3(coeffs.T, jnp.concatenate(rows, 1))
    resid = st_ref[...] - (back[:count, :part] + back[count:, part:])
    resid_ref[...] = resid
    both_ref[: count // 2] = pack(dot3(resid, resid, 1, 1))
    both_ref[count // 2 :] = resid[count // 2 :]


def bundle_back(crossed_ref, rotated_ref, resid_ref, cols_ref, out_ref, cols_out_ref):
    width, half = rotated_ref.shape[1], crossed_ref.shape[1]
    gram = added(crossed_ref)
    out_ref[:, :width] = rotated_ref[...]
    early = resid_ref[:half]
    late = jnp.where(first_core(), resid_ref[half:], gram)
    for j in range(out_ref.shape[0]):
        out_ref[j, width : width + half] = early
        out_ref[j, width + half :] = late
    cols_out_ref[...] = cols_ref[...]


def last(crossed_ref, parts_ref, out_ref):
    modes, half, part = crossed_ref.shape
    out_ref[: modes * half] = crossed_ref[...].reshape(modes * half, part)
    start = parts_ref.shape[1] - half
    total = parts_ref[0, start:]
    for j in range(1, modes):
        total = total + parts_ref[j, start:]
    out_ref[modes * half :] = total


def eliminate(gram):
    count = gram.shape[0]
    tiles = count // STEP
    shape = (STEP, 2 * count)
    lane = lax.broadcasted_iota(jnp.int32, shape, 1)
    sub = lax.broadcasted_iota(jnp.int32, shape, 0)
    wide = jnp.concatenate([gram, jnp.zeros((count, count), jnp.float32)], 1)
    rows = [
        jnp.where(lane == sub + (STEP * t + count), 1.0, wide[STEP * t : STEP * (t + 1)])
        for t in range(tiles)
    ]
    done = []
    for b in range(tiles):
        later = range(b + 1, tiles)
        first = STEP * b
        block = [
            jnp.broadcast_to(rows[b][:, first + k : first + k + 1], shape) for k in range(STEP)
        ]
        column = [
            {t: jnp.broadcast_to(rows[t][:, first + k : first + k + 1], shape) for t in later}
            for k in range(STEP)
        ]
        row = [jnp.broadcast_to(rows[b][k : k + 1], shape) for k in range(STEP)]
        pivot = {
            (i, k): jnp.broadcast_to(block[k][i : i + 1], shape)
            for i in range(STEP)
            for k in range(i + 1)
        }
        scaled = []
        for k in range(STEP):
            inverse = 1.0 / pivot[k, k]
            scaled.append(row[k] * inverse)
            for i in range(k + 1, STEP):
                ratio = pivot[i, k] * inverse
                for m in range(k + 1, i + 1):
                    pivot[i, m] = pivot[i, m] - ratio * pivot[m, k]
                row[i] = row[i] - ratio * row[k]
                for t in later:
                    column[i][t] = column[i][t] - ratio * column[k][t]
        for t in later:
            for k in range(STEP):
                rows[t] = rows[t] - column[k][t] * scaled[k]
        final = jnp.zeros(shape, jnp.float32)
        for k in range(STEP):
            final = jnp.where(sub == k, row[k] * lax.rsqrt(pivot[k, k]), final)
        done.append(jnp.where(lane >= sub + first, final, 0.0))
    return jnp.concatenate(done, 0)


def finish(scale, last_ref, lower_cols_ref, parts_ref, out_ref, factor_ref):
    count, width = lower_cols_ref.shape
    half = count // 2
    modes, _, part = parts_ref.shape
    packed = last_ref[1, modes * half :]
    done = eliminate(jnp.concatenate([packed[:, :count], packed[:, count:]], 0))
    factor_ref[...] = done[:, :count].T * (1.0 / scale)
    weights = dot3(lower_cols_ref[...].T, done[:, count:]) * scale
    for j in range(modes):
        early = parts_ref[j, width : width + half]
        late = jnp.where(
            first_core(), parts_ref[j, width + half :], last_ref[0, j * half : (j + 1) * half]
        )
        resid = jnp.concatenate([early, late], 0)
        out_ref[:, j * part : (j + 1) * part] = parts_ref[j, :width] * scale + dot3(weights, resid)


def kernel(body, out, args, specs=None, scratch=(), params=LIMIT):
    return pl.pallas_call(
        body,
        out_shape=out,
        in_specs=specs or [VMEM] * len(args),
        out_specs=(VMEM,) * len(out) if isinstance(out, tuple) else VMEM,
        scratch_shapes=scratch,
        compiler_params=params,
    )(*args)


def over_space(block, depth):
    both = lax.all_gather(block, CORE, axis=0, tiled=False)
    few = block.shape[0] // 2
    return lax.all_to_all(
        kernel(share, struct(depth, few, block.shape[1]), (both,)), Z, 0, 0, tiled=True
    )


def cross(block, depth, modes):
    devices = np.arange(2 * depth * modes).reshape(depth, 2, modes)
    groups = devices[:, 1].T.tolist() + devices[:, 0].tolist()
    return lax.all_to_all(
        block, (Z, CORE) + MODE, 0, 0, tiled=True, axis_index_groups=groups
    )


def over_cores(block):
    return lax.all_gather(block, CORE, axis=0, tiled=False)


def over_mode(block):
    return lax.all_to_all(block, MODE, 0, 0, tiled=True)


def local(basis, snapshots, rotation):
    depth = lax.axis_size(Z)
    modes = lax.axis_size("y") * lax.axis_size("x")
    rows, width = basis.shape
    count = snapshots.shape[1]
    part = rows // modes
    half = width // 2
    total = rotation.shape[1]
    place = lax.axis_index(MODE)
    scale = float(rows * depth * 2) ** 0.5
    bt, st = basis.T, snapshots.T
    buffers = (
        pltpu.VMEM((width, rows), jnp.float32),
        pltpu.VMEM((count, rows), jnp.float32),
        pltpu.SemaphoreType.DMA((2 * CHUNKS,)),
    )
    first, pieces, st_own = kernel(
        project,
        (struct((modes + 1) * half, part), struct(modes, width, part), struct(count, part)),
        (bt, st),
        [HBM, HBM],
        buffers,
        FULL,
    )
    crossed = kernel(share, struct(depth, half, part), (over_cores(first),))
    crossed = cross(crossed, depth, modes)
    got = over_mode(kernel(bundle, struct(modes, width, part), (crossed, pieces)))
    traded = over_cores(kernel(trade, struct(modes, half, part), (crossed, got)))
    resid, both = kernel(
        remainder, (struct(count, part), struct(2 * half, part)), (got, traded, st_own)
    )
    crossed = kernel(share_back, struct(depth, half, part), (over_cores(both),))
    crossed = cross(crossed, depth, modes)
    later = jnp.where(lax.axis_index(CORE) == 0, got[:, half:], traded[0])
    own = jnp.concatenate([got[:, :half], later], 1).reshape(total, part)
    rotated = dot(rotation[:total], own, 0, 0).reshape(modes, width, part)
    lower_cols = lax.dynamic_slice(rotation, (total, place * width), (count, width))
    pieces, lower_cols = kernel(
        bundle_back,
        (struct(modes, width + count, part), struct(count, width)),
        (crossed, rotated, resid, lower_cols),
    )
    parts = over_mode(pieces)
    gathered = over_cores(kernel(last, struct((modes + 1) * half, part), (crossed, parts)))
    out, factor = kernel(
        functools.partial(finish, scale),
        (struct(width, rows), struct(count, count)),
        (gathered, lower_cols, parts),
    )
    return out.T, factor


def solution(mesh):
    y, x = 4, 4
    split = Mesh(mesh.devices.reshape(-1, 2, y, x), ("z", "core", "y", "x"))
    space, mode = ("z", "core"), ("y", "x")
    placed = (P(space, mode), P(space, None), P())
    return jax.shard_map(
        local, mesh=split, in_specs=placed, out_specs=(P(space, mode), P()), check_vma=False
    )
```

```python
import functools

import jax
import jax.numpy as jnp
import numpy as np
from jax import lax
from jax.experimental import pallas as pl
from jax.experimental.pallas import tpu as pltpu
from jax.sharding import Mesh, PartitionSpec as P

HIGH = lax.Precision.HIGH
Z = "z"
CORE = "core"
MODE = ("y", "x")
STEP = 8
CHUNKS = 4
VMEM = pl.BlockSpec(memory_space=pltpu.VMEM)
HBM = pl.BlockSpec(memory_space=pltpu.HBM)
FULL = pltpu.CompilerParams(vmem_limit_bytes=55_700_000)
LIMIT = pltpu.CompilerParams(vmem_limit_bytes=32 << 20)


def struct(*shape):
    return jax.ShapeDtypeStruct(shape, jnp.float32)


def dot(a, b, left, right):
    return lax.dot_general(a, b, (((left,), (right,)), ((), ())), precision=HIGH)


def halves(a):
    top = a.astype(jnp.bfloat16)
    return top, (a - top.astype(jnp.float32)).astype(jnp.bfloat16)


def dot3(a, b, left=1, right=0):
    (ah, al), (bh, bl) = halves(a), halves(b)

    def one(p, q):
        dims = (((left,), (right,)), ((), ()))
        return lax.dot_general(p, q, dims, preferred_element_type=jnp.float32)

    return one(ah, bh) + (one(ah, bl) + one(al, bh))


def pack(block):
    half = block.shape[0] // 2
    return jnp.concatenate([block[:half], block[half:]], 1)


def pack_symmetric(block):
    half = block.shape[0] // 2
    cut = 3 * half // 4
    quarters = (block[:half, :half], block[half:, :half], block[half:, half:])
    side = jnp.concatenate([quarter[cut:] for quarter in quarters], 0)
    return jnp.concatenate([quarter[:cut] for quarter in quarters] + [side], 1)


def unpack_symmetric(packed):
    half = packed.shape[1] // 4
    step = packed.shape[0] // 3
    first, cross, second = (
        jnp.concatenate(
            [
                packed[:, k * half : (k + 1) * half],
                packed[k * step : (k + 1) * step, 3 * half :],
            ],
            0,
        )
        for k in range(3)
    )
    return jnp.concatenate(
        [jnp.concatenate([first, cross.T], 1), jnp.concatenate([cross, second], 1)], 0
    )


def project(bt_ref, st_ref, first_ref, early_ref, own_ref, b_buf, s_buf, sems):
    step = b_buf.shape[1] // CHUNKS
    copies = []
    for i in range(CHUNKS):
        cut = pl.ds(i * step, step)
        for k, (src, dst) in enumerate(((bt_ref, b_buf), (st_ref, s_buf))):
            copy = pltpu.make_async_copy(src.at[:, cut], dst.at[:, cut], sems.at[2 * i + k])
            copy.start()
            copies.append(copy)
    _, half, part = early_ref.shape
    each = step // part
    total = None
    for i in range(CHUNKS):
        copies[2 * i].wait()
        copies[2 * i + 1].wait()
        cut = slice(i * step, (i + 1) * step)
        basis = b_buf[:, cut]
        term = dot3(basis, s_buf[:, cut], 1, 1)
        total = term if total is None else total + term
        for j in range(i * each, (i + 1) * each):
            piece = b_buf[:, j * part : (j + 1) * part]
            early_ref[j] = piece[:half]
            first_ref[(j + 1) * half : (j + 2) * half] = piece[half:]
    first_ref[:half] = pack(total)
    place = lax.axis_index("y") * lax.axis_size("x") + lax.axis_index("x")
    own_ref[...] = s_buf[:, pl.ds(pl.multiple_of(place * part, part), part)]


def first_core():
    return lax.axis_index(CORE) == 0


def share(both_ref, out_ref):
    count, half, _ = out_ref.shape
    coeffs = both_ref[0, :half] + both_ref[1, :half]
    for k in range(count):
        piece = both_ref[1, (k + 1) * half : (k + 2) * half]
        out_ref[k] = jnp.where(first_core(), piece, coeffs)


def share_back(both_ref, out_ref):
    few = out_ref.shape[1]
    gram = both_ref[0, :few] + both_ref[1, :few]
    mine = jnp.where(first_core(), both_ref[1, few:], gram)
    for k in range(out_ref.shape[0]):
        out_ref[k] = mine


def added(ref):
    total = ref[0]
    for k in range(1, ref.shape[0]):
        total = total + ref[k]
    return total


def bundle(crossed_ref, first_ref, early_ref, out_ref):
    half = crossed_ref.shape[1]
    coeffs = added(crossed_ref)
    out_ref[:, :half] = early_ref[...]
    for j in range(out_ref.shape[0]):
        piece = first_ref[(j + 1) * half : (j + 2) * half]
        out_ref[j, half:] = jnp.where(first_core(), piece, coeffs)


def trade(crossed_ref, got_ref, out_ref):
    half = crossed_ref.shape[1]
    out_ref[...] = jnp.where(first_core(), crossed_ref[...], got_ref[:, half:])


def remainder(got_ref, traded_ref, st_ref, resid_ref, both_ref):
    modes, width, part = got_ref.shape
    count = st_ref.shape[0]
    half = width // 2
    lower = got_ref[:, :half]
    upper = jnp.where(first_core(), got_ref[:, half:], traded_ref[0])
    rows = [block.reshape(modes * half, part) for block in (lower, upper)]
    coeffs = traded_ref[1].reshape(modes * half, 2 * count)
    back = dot3(coeffs.T, jnp.concatenate(rows, 1))
    resid = st_ref[...] - (back[:count, :part] + back[count:, part:])
    resid_ref[...] = resid
    few = both_ref.shape[0] // 2
    both_ref[:few] = pack_symmetric(dot3(resid, resid, 1, 1))
    both_ref[few:] = resid[count - few :]


def bundle_back(crossed_ref, rotated_ref, resid_ref, cols_ref, out_ref, cols_out_ref):
    width, few = rotated_ref.shape[1], crossed_ref.shape[1]
    gram = added(crossed_ref)
    out_ref[:, :width] = rotated_ref[...]
    cut = resid_ref.shape[0] - few
    early = resid_ref[:cut]
    late = jnp.where(first_core(), resid_ref[cut:], gram)
    for j in range(out_ref.shape[0]):
        out_ref[j, width : width + cut] = early
        out_ref[j, width + cut :] = late
    cols_out_ref[...] = cols_ref[...]


def last(crossed_ref, parts_ref, out_ref):
    modes, few, part = crossed_ref.shape
    out_ref[: modes * few] = crossed_ref[...].reshape(modes * few, part)
    start = parts_ref.shape[1] - few
    total = parts_ref[0, start:]
    for j in range(1, modes):
        total = total + parts_ref[j, start:]
    out_ref[modes * few :] = total


def eliminate(gram):
    count = gram.shape[0]
    tiles = count // STEP
    shape = (STEP, 2 * count)
    lane = lax.broadcasted_iota(jnp.int32, shape, 1)
    sub = lax.broadcasted_iota(jnp.int32, shape, 0)
    wide = jnp.concatenate([gram, jnp.zeros((count, count), jnp.float32)], 1)
    rows = [
        jnp.where(lane == sub + (STEP * t + count), 1.0, wide[STEP * t : STEP * (t + 1)])
        for t in range(tiles)
    ]
    done = []
    for b in range(tiles):
        later = range(b + 1, tiles)
        first = STEP * b
        block = [
            jnp.broadcast_to(rows[b][:, first + k : first + k + 1], shape) for k in range(STEP)
        ]
        column = [
            {t: jnp.broadcast_to(rows[t][:, first + k : first + k + 1], shape) for t in later}
            for k in range(STEP)
        ]
        row = [jnp.broadcast_to(rows[b][k : k + 1], shape) for k in range(STEP)]
        pivot = {
            (i, k): jnp.broadcast_to(block[k][i : i + 1], shape)
            for i in range(STEP)
            for k in range(i + 1)
        }
        scaled = []
        for k in range(STEP):
            inverse = 1.0 / pivot[k, k]
            scaled.append(row[k] * inverse)
            for i in range(k + 1, STEP):
                ratio = pivot[i, k] * inverse
                for m in range(k + 1, i + 1):
                    pivot[i, m] = pivot[i, m] - ratio * pivot[m, k]
                row[i] = row[i] - ratio * row[k]
                for t in later:
                    column[i][t] = column[i][t] - ratio * column[k][t]
        for t in later:
            for k in range(STEP):
                rows[t] = rows[t] - column[k][t] * scaled[k]
        final = jnp.zeros(shape, jnp.float32)
        for k in range(STEP):
            final = jnp.where(sub == k, row[k] * lax.rsqrt(pivot[k, k]), final)
        done.append(jnp.where(lane >= sub + first, final, 0.0))
    return jnp.concatenate(done, 0)


def finish(scale, last_ref, lower_cols_ref, parts_ref, out_ref, factor_ref):
    count, width = lower_cols_ref.shape
    modes, _, part = parts_ref.shape
    few = last_ref.shape[1] // (modes + 1)
    cut = width + count - few
    done = eliminate(unpack_symmetric(last_ref[1, modes * few :]))
    factor_ref[...] = done[:, :count].T * (1.0 / scale)
    weights = dot3(lower_cols_ref[...].T, done[:, count:]) * scale
    for j in range(modes):
        late = jnp.where(
            first_core(), parts_ref[j, cut:], last_ref[0, j * few : (j + 1) * few]
        )
        resid = jnp.concatenate([parts_ref[j, width:cut], late], 0)
        out_ref[:, j * part : (j + 1) * part] = parts_ref[j, :width] * scale + dot3(weights, resid)


def kernel(body, out, args, specs=None, scratch=(), params=LIMIT):
    return pl.pallas_call(
        body,
        out_shape=out,
        in_specs=specs or [VMEM] * len(args),
        out_specs=(VMEM,) * len(out) if isinstance(out, tuple) else VMEM,
        scratch_shapes=scratch,
        compiler_params=params,
    )(*args)


def over_space(block, depth):
    both = lax.all_gather(block, CORE, axis=0, tiled=False)
    few = block.shape[0] // 2
    return lax.all_to_all(
        kernel(share, struct(depth, few, block.shape[1]), (both,)), Z, 0, 0, tiled=True
    )


def cross(block, depth, modes):
    devices = np.arange(2 * depth * modes).reshape(depth, 2, modes)
    groups = devices[:, 1].T.tolist() + devices[:, 0].tolist()
    return lax.all_to_all(
        block, (Z, CORE) + MODE, 0, 0, tiled=True, axis_index_groups=groups
    )


def over_cores(block):
    return lax.all_gather(block, CORE, axis=0, tiled=False)


def over_mode(block):
    return lax.all_to_all(block, MODE, 0, 0, tiled=True)


def local(basis, snapshots, rotation):
    depth = lax.axis_size(Z)
    modes = lax.axis_size("y") * lax.axis_size("x")
    rows, width = basis.shape
    count = snapshots.shape[1]
    part = rows // modes
    half = width // 2
    few = 3 * count // 8
    total = rotation.shape[1]
    place = lax.axis_index(MODE)
    scale = float(rows * depth * 2) ** 0.5
    bt, st = basis.T, snapshots.T
    buffers = (
        pltpu.VMEM((width, rows), jnp.float32),
        pltpu.VMEM((count, rows), jnp.float32),
        pltpu.SemaphoreType.DMA((2 * CHUNKS,)),
    )
    first, early, st_own = kernel(
        project,
        (struct((modes + 1) * half, part), struct(modes, half, part), struct(count, part)),
        (bt, st),
        [HBM, HBM],
        buffers,
        FULL,
    )
    crossed = kernel(share, struct(depth, half, part), (over_cores(first),))
    crossed = cross(crossed, depth, modes)
    got = over_mode(kernel(bundle, struct(modes, width, part), (crossed, first, early)))
    traded = over_cores(kernel(trade, struct(modes, half, part), (crossed, got)))
    resid, both = kernel(
        remainder, (struct(count, part), struct(2 * few, part)), (got, traded, st_own)
    )
    crossed = kernel(share_back, struct(depth, few, part), (over_cores(both),))
    crossed = cross(crossed, depth, modes)
    later = jnp.where(lax.axis_index(CORE) == 0, got[:, half:], traded[0])
    own = jnp.concatenate([got[:, :half], later], 1).reshape(total, part)
    rotated = dot(rotation[:total], own, 0, 0).reshape(modes, width, part)
    lower_cols = lax.dynamic_slice(rotation, (total, place * width), (count, width))
    pieces, lower_cols = kernel(
        bundle_back,
        (struct(modes, width + count, part), struct(count, width)),
        (crossed, rotated, resid, lower_cols),
    )
    parts = over_mode(pieces)
    gathered = over_cores(kernel(last, struct((modes + 1) * few, part), (crossed, parts)))
    out, factor = kernel(
        functools.partial(finish, scale),
        (struct(width, rows), struct(count, count)),
        (gathered, lower_cols, parts),
    )
    return out.T, factor


def solution(mesh):
    y, x = 4, 4
    split = Mesh(mesh.devices.reshape(-1, 2, y, x), ("z", "core", "y", "x"))
    space, mode = ("z", "core"), ("y", "x")
    placed = (P(space, mode), P(space, None), P())
    return jax.shard_map(
        local, mesh=split, in_specs=placed, out_specs=(P(space, mode), P()), check_vma=False
    )
```

```python
import functools

import jax
import jax.numpy as jnp
import numpy as np
from jax import lax
from jax.experimental import pallas as pl
from jax.experimental.pallas import tpu as pltpu
from jax.sharding import Mesh, PartitionSpec as P

HIGH = lax.Precision.HIGH
Z = "z"
CORE = "core"
MODE = ("y", "x")
STEP = 8
CHUNKS = 4
VMEM = pl.BlockSpec(memory_space=pltpu.VMEM)
HBM = pl.BlockSpec(memory_space=pltpu.HBM)
FULL = pltpu.CompilerParams(vmem_limit_bytes=55_700_000)
LIMIT = pltpu.CompilerParams(vmem_limit_bytes=32 << 20)


def struct(*shape):
    return jax.ShapeDtypeStruct(shape, jnp.float32)


def dot(a, b, left, right):
    return lax.dot_general(a, b, (((left,), (right,)), ((), ())), precision=HIGH)


def halves(a):
    top = a.astype(jnp.bfloat16)
    return top, (a - top.astype(jnp.float32)).astype(jnp.bfloat16)


def dot3(a, b, left=1, right=0):
    (ah, al), (bh, bl) = halves(a), halves(b)

    def one(p, q):
        dims = (((left,), (right,)), ((), ()))
        return lax.dot_general(p, q, dims, preferred_element_type=jnp.float32)

    return one(ah, bh) + (one(ah, bl) + one(al, bh))


def pack(block):
    half = block.shape[0] // 2
    return jnp.concatenate([block[:half], block[half:]], 1)


def pack_symmetric(block):
    half = block.shape[0] // 2
    cut = 3 * half // 4
    quarters = (block[:half, :half], block[half:, :half], block[half:, half:])
    side = jnp.concatenate([quarter[cut:] for quarter in quarters], 0)
    return jnp.concatenate([quarter[:cut] for quarter in quarters] + [side], 1)


def unpack_symmetric(packed):
    half = packed.shape[1] // 4
    step = packed.shape[0] // 3
    first, cross, second = (
        jnp.concatenate(
            [
                packed[:, k * half : (k + 1) * half],
                packed[k * step : (k + 1) * step, 3 * half :],
            ],
            0,
        )
        for k in range(3)
    )
    return jnp.concatenate(
        [jnp.concatenate([first, cross.T], 1), jnp.concatenate([cross, second], 1)], 0
    )


def project(
    bt_ref, st_ref, rot_ref, first_ref, early_ref, own_ref, cols_ref, b_buf, s_buf, r_buf, sems
):
    step = b_buf.shape[1] // CHUNKS
    copies = []
    for i in range(CHUNKS):
        cut = pl.ds(i * step, step)
        for k, (src, dst) in enumerate(((bt_ref, b_buf), (st_ref, s_buf))):
            copy = pltpu.make_async_copy(src.at[:, cut], dst.at[:, cut], sems.at[2 * i + k])
            copy.start()
            copies.append(copy)
    _, half, part = early_ref.shape
    each = step // part
    place = lax.axis_index("y") * lax.axis_size("x") + lax.axis_index("x")
    count, width = cols_ref.shape
    wide = r_buf.shape[1]
    side = pl.ds(pl.multiple_of(place // (wide // width) * wide, wide), wide)
    columns = pltpu.make_async_copy(
        rot_ref.at[pl.ds(rot_ref.shape[0] - count, count), side], r_buf, sems.at[2 * CHUNKS]
    )
    columns.start()
    total = None
    for i in range(CHUNKS):
        copies[2 * i].wait()
        copies[2 * i + 1].wait()
        cut = slice(i * step, (i + 1) * step)
        basis = b_buf[:, cut]
        term = dot3(basis, s_buf[:, cut], 1, 1)
        total = term if total is None else total + term
        for j in range(i * each, (i + 1) * each):
            piece = b_buf[:, j * part : (j + 1) * part]
            early_ref[j] = piece[:half]
            first_ref[(j + 1) * half : (j + 2) * half] = piece[half:]
    first_ref[:half] = pack(total)
    own_ref[...] = s_buf[:, pl.ds(pl.multiple_of(place * part, part), part)]
    columns.wait()
    found = r_buf[...]
    cols_ref[...] = jnp.where(place % 2 == 0, found[:, :width], found[:, width:])


def first_core():
    return lax.axis_index(CORE) == 0


def share(both_ref, out_ref):
    count, half, _ = out_ref.shape
    coeffs = both_ref[0, :half] + both_ref[1, :half]
    for k in range(count):
        piece = both_ref[1, (k + 1) * half : (k + 2) * half]
        out_ref[k] = jnp.where(first_core(), piece, coeffs)


def share_back(both_ref, out_ref):
    few = out_ref.shape[1]
    gram = both_ref[0, :few] + both_ref[1, :few]
    mine = jnp.where(first_core(), both_ref[1, few:], gram)
    for k in range(out_ref.shape[0]):
        out_ref[k] = mine


def added(ref):
    total = ref[0]
    for k in range(1, ref.shape[0]):
        total = total + ref[k]
    return total


def bundle(crossed_ref, first_ref, early_ref, out_ref):
    half = crossed_ref.shape[1]
    coeffs = added(crossed_ref)
    out_ref[:, :half] = early_ref[...]
    for j in range(out_ref.shape[0]):
        piece = first_ref[(j + 1) * half : (j + 2) * half]
        out_ref[j, half:] = jnp.where(first_core(), piece, coeffs)


def trade(crossed_ref, got_ref, out_ref):
    half = crossed_ref.shape[1]
    out_ref[...] = jnp.where(first_core(), crossed_ref[...], got_ref[:, half:])


def remainder(got_ref, traded_ref, st_ref, resid_ref, both_ref):
    modes, width, part = got_ref.shape
    count = st_ref.shape[0]
    half = width // 2
    lower = got_ref[:, :half]
    upper = jnp.where(first_core(), got_ref[:, half:], traded_ref[0])
    rows = [block.reshape(modes * half, part) for block in (lower, upper)]
    coeffs = traded_ref[1].reshape(modes * half, 2 * count)
    back = dot3(coeffs.T, jnp.concatenate(rows, 1))
    resid = st_ref[...] - (back[:count, :part] + back[count:, part:])
    resid_ref[...] = resid
    few = both_ref.shape[0] // 2
    both_ref[:few] = pack_symmetric(dot3(resid, resid, 1, 1))
    both_ref[few:] = resid[count - few :]


def bundle_back(crossed_ref, rotated_ref, resid_ref, out_ref):
    width, few = rotated_ref.shape[1], crossed_ref.shape[1]
    gram = added(crossed_ref)
    out_ref[:, :width] = rotated_ref[...]
    cut = resid_ref.shape[0] - few
    early = resid_ref[:cut]
    late = jnp.where(first_core(), resid_ref[cut:], gram)
    for j in range(out_ref.shape[0]):
        out_ref[j, width : width + cut] = early
        out_ref[j, width + cut :] = late


def last(crossed_ref, parts_ref, out_ref):
    modes, few, part = crossed_ref.shape
    out_ref[: modes * few] = crossed_ref[...].reshape(modes * few, part)
    start = parts_ref.shape[1] - few
    total = parts_ref[0, start:]
    for j in range(1, modes):
        total = total + parts_ref[j, start:]
    out_ref[modes * few :] = total


def eliminate(gram):
    count = gram.shape[0]
    tiles = count // STEP
    shape = (STEP, 2 * count)
    lane = lax.broadcasted_iota(jnp.int32, shape, 1)
    sub = lax.broadcasted_iota(jnp.int32, shape, 0)
    wide = jnp.concatenate([gram, jnp.zeros((count, count), jnp.float32)], 1)
    rows = [
        jnp.where(lane == sub + (STEP * t + count), 1.0, wide[STEP * t : STEP * (t + 1)])
        for t in range(tiles)
    ]
    done = []
    for b in range(tiles):
        later = range(b + 1, tiles)
        first = STEP * b
        block = [
            jnp.broadcast_to(rows[b][:, first + k : first + k + 1], shape) for k in range(STEP)
        ]
        column = [
            {t: jnp.broadcast_to(rows[t][:, first + k : first + k + 1], shape) for t in later}
            for k in range(STEP)
        ]
        row = [jnp.broadcast_to(rows[b][k : k + 1], shape) for k in range(STEP)]
        pivot = {
            (i, k): jnp.broadcast_to(block[k][i : i + 1], shape)
            for i in range(STEP)
            for k in range(i + 1)
        }
        scaled = []
        for k in range(STEP):
            inverse = 1.0 / pivot[k, k]
            scaled.append(row[k] * inverse)
            for i in range(k + 1, STEP):
                ratio = pivot[i, k] * inverse
                for m in range(k + 1, i + 1):
                    pivot[i, m] = pivot[i, m] - ratio * pivot[m, k]
                row[i] = row[i] - ratio * row[k]
                for t in later:
                    column[i][t] = column[i][t] - ratio * column[k][t]
        for t in later:
            for k in range(STEP):
                rows[t] = rows[t] - column[k][t] * scaled[k]
        final = jnp.zeros(shape, jnp.float32)
        for k in range(STEP):
            final = jnp.where(sub == k, row[k] * lax.rsqrt(pivot[k, k]), final)
        done.append(jnp.where(lane >= sub + first, final, 0.0))
    return jnp.concatenate(done, 0)


def finish(scale, last_ref, lower_cols_ref, parts_ref, out_ref, factor_ref):
    count, width = lower_cols_ref.shape
    modes, _, part = parts_ref.shape
    few = last_ref.shape[1] // (modes + 1)
    cut = width + count - few
    done = eliminate(unpack_symmetric(last_ref[1, modes * few :]))
    factor_ref[...] = done[:, :count].T * (1.0 / scale)
    weights = dot3(lower_cols_ref[...].T, done[:, count:]) * scale
    for j in range(modes):
        late = jnp.where(
            first_core(), parts_ref[j, cut:], last_ref[0, j * few : (j + 1) * few]
        )
        resid = jnp.concatenate([parts_ref[j, width:cut], late], 0)
        out_ref[:, j * part : (j + 1) * part] = parts_ref[j, :width] * scale + dot3(weights, resid)


def kernel(body, out, args, specs=None, scratch=(), params=LIMIT):
    return pl.pallas_call(
        body,
        out_shape=out,
        in_specs=specs or [VMEM] * len(args),
        out_specs=(VMEM,) * len(out) if isinstance(out, tuple) else VMEM,
        scratch_shapes=scratch,
        compiler_params=params,
    )(*args)


def over_space(block, depth):
    both = lax.all_gather(block, CORE, axis=0, tiled=False)
    few = block.shape[0] // 2
    return lax.all_to_all(
        kernel(share, struct(depth, few, block.shape[1]), (both,)), Z, 0, 0, tiled=True
    )


def cross(block, depth, modes):
    devices = np.arange(2 * depth * modes).reshape(depth, 2, modes)
    groups = devices[:, 1].T.tolist() + devices[:, 0].tolist()
    return lax.all_to_all(
        block, (Z, CORE) + MODE, 0, 0, tiled=True, axis_index_groups=groups
    )


def over_cores(block):
    return lax.all_gather(block, CORE, axis=0, tiled=False)


def over_mode(block):
    return lax.all_to_all(block, MODE, 0, 0, tiled=True)


def local(basis, snapshots, rotation):
    depth = lax.axis_size(Z)
    modes = lax.axis_size("y") * lax.axis_size("x")
    rows, width = basis.shape
    count = snapshots.shape[1]
    part = rows // modes
    half = width // 2
    few = 3 * count // 8
    total = rotation.shape[1]
    scale = float(rows * depth * 2) ** 0.5
    bt, st = basis.T, snapshots.T
    buffers = (
        pltpu.VMEM((width, rows), jnp.float32),
        pltpu.VMEM((count, rows), jnp.float32),
        pltpu.VMEM((count, 2 * width), jnp.float32),
        pltpu.SemaphoreType.DMA((2 * CHUNKS + 1,)),
    )
    first, early, st_own, lower_cols = kernel(
        project,
        (
            struct((modes + 1) * half, part),
            struct(modes, half, part),
            struct(count, part),
            struct(count, width),
        ),
        (bt, st, rotation),
        [HBM] * 3,
        buffers,
        FULL,
    )
    crossed = kernel(share, struct(depth, half, part), (over_cores(first),))
    crossed = cross(crossed, depth, modes)
    got = over_mode(kernel(bundle, struct(modes, width, part), (crossed, first, early)))
    traded = over_cores(kernel(trade, struct(modes, half, part), (crossed, got)))
    resid, both = kernel(
        remainder, (struct(count, part), struct(2 * few, part)), (got, traded, st_own)
    )
    crossed = kernel(share_back, struct(depth, few, part), (over_cores(both),))
    crossed = cross(crossed, depth, modes)
    later = jnp.where(lax.axis_index(CORE) == 0, got[:, half:], traded[0])
    own = jnp.concatenate([got[:, :half], later], 1).reshape(total, part)
    rotated = dot(rotation[:total], own, 0, 0).reshape(modes, width, part)
    pieces = kernel(
        bundle_back, struct(modes, width + count, part), (crossed, rotated, resid)
    )
    parts = over_mode(pieces)
    gathered = over_cores(kernel(last, struct((modes + 1) * few, part), (crossed, parts)))
    out, factor = kernel(
        functools.partial(finish, scale),
        (struct(width, rows), struct(count, count)),
        (gathered, lower_cols, parts),
    )
    return out.T, factor


def solution(mesh):
    y, x = 4, 4
    split = Mesh(mesh.devices.reshape(-1, 2, y, x), ("z", "core", "y", "x"))
    space, mode = ("z", "core"), ("y", "x")
    placed = (P(space, mode), P(space, None), P())
    return jax.shard_map(
        local, mesh=split, in_specs=placed, out_specs=(P(space, mode), P()), check_vma=False
    )
```

```python
import functools

import jax
import jax.numpy as jnp
import numpy as np
from jax import lax
from jax.experimental import pallas as pl
from jax.experimental.pallas import tpu as pltpu
from jax.sharding import Mesh, PartitionSpec as P

HIGH = lax.Precision.HIGH
Z = "z"
CORE = "core"
MODE = ("y", "x")
STEP = 8
CHUNKS = 4
VMEM = pl.BlockSpec(memory_space=pltpu.VMEM)
HBM = pl.BlockSpec(memory_space=pltpu.HBM)
FULL = pltpu.CompilerParams(vmem_limit_bytes=55_700_000)
LIMIT = pltpu.CompilerParams(vmem_limit_bytes=32 << 20)


def struct(*shape):
    return jax.ShapeDtypeStruct(shape, jnp.float32)


def dot(a, b, left, right):
    return lax.dot_general(a, b, (((left,), (right,)), ((), ())), precision=HIGH)


def halves(a):
    top = a.astype(jnp.bfloat16)
    return top, (a - top.astype(jnp.float32)).astype(jnp.bfloat16)


def dot3(a, b, left=1, right=0):
    (ah, al), (bh, bl) = halves(a), halves(b)

    def one(p, q):
        dims = (((left,), (right,)), ((), ()))
        return lax.dot_general(p, q, dims, preferred_element_type=jnp.float32)

    return one(ah, bh) + (one(ah, bl) + one(al, bh))


def pack(block):
    half = block.shape[0] // 2
    return jnp.concatenate([block[:half], block[half:]], 1)


def square(size):
    return [lax.broadcasted_iota(jnp.int32, (size, size), d) for d in range(2)]


def pack_symmetric(block):
    half = block.shape[0] // 2
    step = half // 2
    row, col = square(half)
    last_quarter = block[half:, half:]
    mixed = jnp.where(row >= col, block[:half, :half], last_quarter)
    cross = block[half:, :half]
    diagonal = jnp.sum(jnp.where(row == col, last_quarter, 0.0), 0, keepdims=True)
    top = [mixed[:step], mixed[step:], cross[:step], cross[step:]]
    rest = [jnp.broadcast_to(diagonal, (8, half)), jnp.zeros((8, 3 * half), jnp.float32)]
    return jnp.concatenate([jnp.concatenate(top, 1), jnp.concatenate(rest, 1)], 0)


def unpack_symmetric(packed):
    half = packed.shape[1] // 4
    step = half // 2
    row, col = square(half)
    mixed, cross = (
        jnp.concatenate(
            [packed[:step, k * half : (k + 1) * half] for k in (first, first + 1)], 0
        )
        for first in (0, 2)
    )
    turned = mixed.T
    first = jnp.where(row >= col, mixed, turned)
    last_quarter = jnp.where(row < col, mixed, turned)
    diagonal = jnp.broadcast_to(packed[step : step + 1, :half], (half, half))
    last_quarter = jnp.where(row == col, diagonal, last_quarter)
    return jnp.concatenate(
        [jnp.concatenate([first, cross.T], 1), jnp.concatenate([cross, last_quarter], 1)], 0
    )


def project(
    bt_ref, st_ref, rot_ref, first_ref, early_ref, own_ref, cols_ref, b_buf, s_buf, r_buf, sems
):
    step = b_buf.shape[1] // CHUNKS
    copies = []
    for i in range(CHUNKS):
        cut = pl.ds(i * step, step)
        for k, (src, dst) in enumerate(((bt_ref, b_buf), (st_ref, s_buf))):
            copy = pltpu.make_async_copy(src.at[:, cut], dst.at[:, cut], sems.at[2 * i + k])
            copy.start()
            copies.append(copy)
    _, half, part = early_ref.shape
    each = step // part
    place = lax.axis_index("y") * lax.axis_size("x") + lax.axis_index("x")
    count, width = cols_ref.shape
    wide = r_buf.shape[1]
    side = pl.ds(pl.multiple_of(place // (wide // width) * wide, wide), wide)
    columns = pltpu.make_async_copy(
        rot_ref.at[pl.ds(rot_ref.shape[0] - count, count), side], r_buf, sems.at[2 * CHUNKS]
    )
    columns.start()
    total = None
    for i in range(CHUNKS):
        copies[2 * i].wait()
        copies[2 * i + 1].wait()
        cut = slice(i * step, (i + 1) * step)
        basis = b_buf[:, cut]
        term = dot3(basis, s_buf[:, cut], 1, 1)
        total = term if total is None else total + term
        for j in range(i * each, (i + 1) * each):
            piece = b_buf[:, j * part : (j + 1) * part]
            early_ref[j] = piece[:half]
            first_ref[(j + 1) * half : (j + 2) * half] = piece[half:]
    first_ref[:half] = pack(total)
    own_ref[...] = s_buf[:, pl.ds(pl.multiple_of(place * part, part), part)]
    columns.wait()
    found = r_buf[...]
    cols_ref[...] = jnp.where(place % 2 == 0, found[:, :width], found[:, width:])


def first_core():
    return lax.axis_index(CORE) == 0


def share(both_ref, out_ref):
    count, half, _ = out_ref.shape
    coeffs = both_ref[0, :half] + both_ref[1, :half]
    for k in range(count):
        piece = both_ref[1, (k + 1) * half : (k + 2) * half]
        out_ref[k] = jnp.where(first_core(), piece, coeffs)


def flat(block, first, used):
    return jnp.concatenate([block[r : r + 1] for r in range(first, first + used)], 1)


def stacked(row, part, above, below):
    pieces = [row[:, r : r + part] for r in range(0, row.shape[1], part)]
    if above:
        pieces = [jnp.zeros((above, part), jnp.float32)] + pieces
    if below:
        pieces = pieces + [jnp.zeros((below, part), jnp.float32)]
    return jnp.concatenate(pieces, 0)


def patched(block, spare, rows):
    place = lax.broadcasted_iota(jnp.int32, block.shape, 0)
    return jnp.where(first_core(), block, jnp.where(place < spare, block, rows))


def share_back(both_ref, out_ref):
    few = both_ref.shape[1] // 2
    used = out_ref.shape[2] // both_ref.shape[2]
    gram = both_ref[0, :few] + both_ref[1, :few]
    late = both_ref[1, few:]
    row = jnp.where(first_core(), flat(late, few - used, used), flat(gram, 0, used))
    for k in range(out_ref.shape[0]):
        out_ref[k] = row


def added(ref, start=0):
    total = ref[0, start:]
    for k in range(1, ref.shape[0]):
        total = total + ref[k, start:]
    return total


def bundle(crossed_ref, first_ref, early_ref, out_ref):
    half = crossed_ref.shape[1]
    coeffs = added(crossed_ref)
    out_ref[:, :half] = early_ref[...]
    for j in range(out_ref.shape[0]):
        piece = first_ref[(j + 1) * half : (j + 2) * half]
        out_ref[j, half:] = jnp.where(first_core(), piece, coeffs)


def trade(crossed_ref, got_ref, out_ref):
    half = crossed_ref.shape[1]
    out_ref[...] = jnp.where(first_core(), crossed_ref[...], got_ref[:, half:])


def join(got_ref, traded_ref, out_ref):
    half = traded_ref.shape[2]
    late = jnp.where(first_core(), got_ref[:, half:], traded_ref[0])
    rows = jnp.concatenate([got_ref[:, :half], late], 1)
    out_ref[...] = rows.reshape(out_ref.shape)


def remainder(got_ref, traded_ref, st_ref, resid_ref, both_ref):
    modes, width, part = got_ref.shape
    count = st_ref.shape[0]
    half = width // 2
    lower = got_ref[:, :half]
    upper = jnp.where(first_core(), got_ref[:, half:], traded_ref[0])
    rows = [block.reshape(modes * half, part) for block in (lower, upper)]
    coeffs = traded_ref[1].reshape(modes * half, 2 * count)
    back = dot3(coeffs.T, jnp.concatenate(rows, 1))
    resid = st_ref[...] - (back[:count, :part] + back[count:, part:])
    resid_ref[...] = resid
    few = both_ref.shape[0] // 2
    both_ref[:few] = pack_symmetric(dot3(resid, resid, 1, 1))
    both_ref[few:] = resid[count - few :]


def bundle_back(crossed_ref, rotated_ref, resid_ref, out_ref):
    modes, width, part = rotated_ref.shape
    count = resid_ref.shape[0]
    used = crossed_ref.shape[2] // part
    few = (used + 7) // 8 * 8
    gram = stacked(added(crossed_ref), part, few - used, 0)
    early = resid_ref[: count - few]
    late = patched(resid_ref[count - few :], few - used, gram)
    out_ref[:, :width] = rotated_ref[...]
    for j in range(modes):
        out_ref[j, width : width + count - few] = early
        out_ref[j, width + count - few :] = late


def last(crossed_ref, parts_ref, out_ref):
    modes = crossed_ref.shape[0]
    used = crossed_ref.shape[2] // parts_ref.shape[2]
    few = (used + 7) // 8 * 8
    out_ref[:modes] = crossed_ref[...]
    gram = added(parts_ref, parts_ref.shape[1] - few)
    out_ref[modes] = flat(gram, few - used, used)


def eliminate(gram):
    count = gram.shape[0]
    tiles = count // STEP
    shape = (STEP, 2 * count)
    lane = lax.broadcasted_iota(jnp.int32, shape, 1)
    sub = lax.broadcasted_iota(jnp.int32, shape, 0)
    wide = jnp.concatenate([gram, jnp.zeros((count, count), jnp.float32)], 1)
    rows = [
        jnp.where(lane == sub + (STEP * t + count), 1.0, wide[STEP * t : STEP * (t + 1)])
        for t in range(tiles)
    ]
    done = []
    for b in range(tiles):
        later = range(b + 1, tiles)
        first = STEP * b
        block = [
            jnp.broadcast_to(rows[b][:, first + k : first + k + 1], shape) for k in range(STEP)
        ]
        column = [
            {t: jnp.broadcast_to(rows[t][:, first + k : first + k + 1], shape) for t in later}
            for k in range(STEP)
        ]
        row = [jnp.broadcast_to(rows[b][k : k + 1], shape) for k in range(STEP)]
        pivot = {
            (i, k): jnp.broadcast_to(block[k][i : i + 1], shape)
            for i in range(STEP)
            for k in range(i + 1)
        }
        scaled = []
        for k in range(STEP):
            inverse = 1.0 / pivot[k, k]
            scaled.append(row[k] * inverse)
            for i in range(k + 1, STEP):
                ratio = pivot[i, k] * inverse
                for m in range(k + 1, i + 1):
                    pivot[i, m] = pivot[i, m] - ratio * pivot[m, k]
                row[i] = row[i] - ratio * row[k]
                for t in later:
                    column[i][t] = column[i][t] - ratio * column[k][t]
        for t in later:
            for k in range(STEP):
                rows[t] = rows[t] - column[k][t] * scaled[k]
        final = jnp.zeros(shape, jnp.float32)
        for k in range(STEP):
            final = jnp.where(sub == k, row[k] * lax.rsqrt(pivot[k, k]), final)
        done.append(jnp.where(lane >= sub + first, final, 0.0))
    return jnp.concatenate(done, 0)


def finish(scale, last_ref, lower_cols_ref, parts_ref, out_ref, factor_ref):
    count, width = lower_cols_ref.shape
    modes, _, part = parts_ref.shape
    used = last_ref.shape[3] // part
    few = (used + 7) // 8 * 8
    cut = width + count - few
    gram = stacked(last_ref[1, modes], part, 0, few - used)
    done = eliminate(unpack_symmetric(gram))
    factor_ref[...] = done[:, :count].T * (1.0 / scale)
    weights = dot3(lower_cols_ref[...].T, done[:, count:]) * scale
    for j in range(modes):
        late = stacked(last_ref[0, j], part, few - used, 0)
        late = patched(parts_ref[j, cut:], few - used, late)
        resid = jnp.concatenate([parts_ref[j, width:cut], late], 0)
        out_ref[:, j * part : (j + 1) * part] = parts_ref[j, :width] * scale + dot3(weights, resid)


def kernel(body, out, args, specs=None, scratch=(), params=LIMIT):
    return pl.pallas_call(
        body,
        out_shape=out,
        in_specs=specs or [VMEM] * len(args),
        out_specs=(VMEM,) * len(out) if isinstance(out, tuple) else VMEM,
        scratch_shapes=scratch,
        compiler_params=params,
    )(*args)


def over_space(block, depth):
    both = lax.all_gather(block, CORE, axis=0, tiled=False)
    few = block.shape[0] // 2
    return lax.all_to_all(
        kernel(share, struct(depth, few, block.shape[1]), (both,)), Z, 0, 0, tiled=True
    )


def cross(block, depth, modes):
    devices = np.arange(2 * depth * modes).reshape(depth, 2, modes)
    groups = devices[:, 1].T.tolist() + devices[:, 0].tolist()
    return lax.all_to_all(
        block, (Z, CORE) + MODE, 0, 0, tiled=True, axis_index_groups=groups
    )


def over_cores(block):
    return lax.all_gather(block, CORE, axis=0, tiled=False)


def over_mode(block):
    return lax.all_to_all(block, MODE, 0, 0, tiled=True)


def local(basis, snapshots, rotation):
    depth = lax.axis_size(Z)
    modes = lax.axis_size("y") * lax.axis_size("x")
    rows, width = basis.shape
    count = snapshots.shape[1]
    part = rows // modes
    half = width // 2
    few = 3 * count // 8
    used = count // 4 + 1
    total = rotation.shape[1]
    scale = float(rows * depth * 2) ** 0.5
    bt, st = basis.T, snapshots.T
    buffers = (
        pltpu.VMEM((width, rows), jnp.float32),
        pltpu.VMEM((count, rows), jnp.float32),
        pltpu.VMEM((count, 2 * width), jnp.float32),
        pltpu.SemaphoreType.DMA((2 * CHUNKS + 1,)),
    )
    first, early, st_own, lower_cols = kernel(
        project,
        (
            struct((modes + 1) * half, part),
            struct(modes, half, part),
            struct(count, part),
            struct(count, width),
        ),
        (bt, st, rotation),
        [HBM] * 3,
        buffers,
        FULL,
    )
    crossed = kernel(share, struct(depth, half, part), (over_cores(first),))
    crossed = cross(crossed, depth, modes)
    got = over_mode(kernel(bundle, struct(modes, width, part), (crossed, first, early)))
    traded = over_cores(kernel(trade, struct(modes, half, part), (crossed, got)))
    resid, both = kernel(
        remainder, (struct(count, part), struct(2 * few, part)), (got, traded, st_own)
    )
    crossed = kernel(share_back, struct(depth, 1, used * part), (over_cores(both),))
    crossed = cross(crossed, depth, modes)
    own = kernel(join, struct(total, part), (got, traded))
    rotated = dot(rotation[:total], own, 0, 0).reshape(modes, width, part)
    pieces = kernel(
        bundle_back, struct(modes, width + count, part), (crossed, rotated, resid)
    )
    parts = over_mode(pieces)
    gathered = over_cores(kernel(last, struct(modes + 1, 1, used * part), (crossed, parts)))
    out, factor = kernel(
        functools.partial(finish, scale),
        (struct(width, rows), struct(count, count)),
        (gathered, lower_cols, parts),
    )
    return out.T, factor


def solution(mesh):
    y, x = 4, 4
    split = Mesh(mesh.devices.reshape(-1, 2, y, x), ("z", "core", "y", "x"))
    space, mode = ("z", "core"), ("y", "x")
    placed = (P(space, mode), P(space, None), P())
    return jax.shard_map(
        local, mesh=split, in_specs=placed, out_specs=(P(space, mode), P()), check_vma=False
    )
```

```python
import functools

import jax
import jax.numpy as jnp
import numpy as np
from jax import lax
from jax.experimental import pallas as pl
from jax.experimental.pallas import tpu as pltpu
from jax.sharding import Mesh, PartitionSpec as P

HIGH = lax.Precision.HIGH
Z = "z"
CORE = "core"
MODE = ("y", "x")
STEP = 8
CHUNKS = 4
VMEM = pl.BlockSpec(memory_space=pltpu.VMEM)
HBM = pl.BlockSpec(memory_space=pltpu.HBM)
FULL = pltpu.CompilerParams(vmem_limit_bytes=55_700_000)
LIMIT = pltpu.CompilerParams(vmem_limit_bytes=32 << 20)


def struct(*shape):
    return jax.ShapeDtypeStruct(shape, jnp.float32)


def dot(a, b, left, right):
    return lax.dot_general(a, b, (((left,), (right,)), ((), ())), precision=HIGH)


def halves(a):
    top = a.astype(jnp.bfloat16)
    return top, (a - top.astype(jnp.float32)).astype(jnp.bfloat16)


def dot3(a, b, left=1, right=0):
    (ah, al), (bh, bl) = halves(a), halves(b)

    def one(p, q):
        dims = (((left,), (right,)), ((), ()))
        return lax.dot_general(p, q, dims, preferred_element_type=jnp.float32)

    return one(ah, bh) + (one(ah, bl) + one(al, bh))


def pack(block):
    half = block.shape[0] // 2
    return jnp.concatenate([block[:half], block[half:]], 1)


def square(size):
    return [lax.broadcasted_iota(jnp.int32, (size, size), d) for d in range(2)]


def pack_symmetric(block):
    half = block.shape[0] // 2
    step = half // 2
    row, col = square(half)
    last_quarter = block[half:, half:]
    mixed = jnp.where(row >= col, block[:half, :half], last_quarter)
    cross = block[half:, :half]
    diagonal = jnp.sum(jnp.where(row == col, last_quarter, 0.0), 0, keepdims=True)
    top = [mixed[:step], mixed[step:], cross[:step], cross[step:]]
    rest = [jnp.broadcast_to(diagonal, (8, half)), jnp.zeros((8, 3 * half), jnp.float32)]
    return jnp.concatenate([jnp.concatenate(top, 1), jnp.concatenate(rest, 1)], 0)


def unpack_symmetric(packed):
    half = packed.shape[1] // 4
    step = half // 2
    row, col = square(half)
    mixed, cross = (
        jnp.concatenate(
            [packed[:step, k * half : (k + 1) * half] for k in (first, first + 1)], 0
        )
        for first in (0, 2)
    )
    turned = mixed.T
    first = jnp.where(row >= col, mixed, turned)
    last_quarter = jnp.where(row < col, mixed, turned)
    diagonal = jnp.broadcast_to(packed[step : step + 1, :half], (half, half))
    last_quarter = jnp.where(row == col, diagonal, last_quarter)
    return jnp.concatenate(
        [jnp.concatenate([first, cross.T], 1), jnp.concatenate([cross, last_quarter], 1)], 0
    )


def project(
    bt_ref, st_ref, rot_ref, first_ref, early_ref, own_ref, cols_ref, b_buf, s_buf, r_buf, sems
):
    step = b_buf.shape[1] // CHUNKS
    copies = []
    for i in range(CHUNKS):
        cut = pl.ds(i * step, step)
        for k, (src, dst) in enumerate(((bt_ref, b_buf), (st_ref, s_buf))):
            copy = pltpu.make_async_copy(src.at[:, cut], dst.at[:, cut], sems.at[2 * i + k])
            copy.start()
            copies.append(copy)
    _, half, part = early_ref.shape
    each = step // part
    place = lax.axis_index("y") * lax.axis_size("x") + lax.axis_index("x")
    count, width = cols_ref.shape
    wide = r_buf.shape[1]
    side = pl.ds(pl.multiple_of(place // (wide // width) * wide, wide), wide)
    columns = pltpu.make_async_copy(
        rot_ref.at[pl.ds(rot_ref.shape[0] - count, count), side], r_buf, sems.at[2 * CHUNKS]
    )
    columns.start()
    total = None
    for i in range(CHUNKS):
        copies[2 * i].wait()
        copies[2 * i + 1].wait()
        cut = slice(i * step, (i + 1) * step)
        basis = b_buf[:, cut]
        term = dot3(basis, s_buf[:, cut], 1, 1)
        total = term if total is None else total + term
        for j in range(i * each, (i + 1) * each):
            piece = b_buf[:, j * part : (j + 1) * part]
            early_ref[j] = piece[:half]
            first_ref[(j + 1) * half : (j + 2) * half] = piece[half:]
    first_ref[:half] = pack(total)
    own_ref[...] = s_buf[:, pl.ds(pl.multiple_of(place * part, part), part)]
    columns.wait()
    found = r_buf[...]
    cols_ref[...] = jnp.where(place % 2 == 0, found[:, :width], found[:, width:])


def first_core():
    return lax.axis_index(CORE) == 0


def share(both_ref, out_ref):
    count, half, _ = out_ref.shape
    coeffs = both_ref[0, :half] + both_ref[1, :half]
    for k in range(count):
        piece = both_ref[0, (k + 1) * half : (k + 2) * half]
        out_ref[k] = jnp.where(first_core(), piece, coeffs)


def flat(block, first, used):
    return jnp.concatenate([block[r : r + 1] for r in range(first, first + used)], 1)


def stacked(row, part, above, below):
    pieces = [row[:, r : r + part] for r in range(0, row.shape[1], part)]
    if above:
        pieces = [jnp.zeros((above, part), jnp.float32)] + pieces
    if below:
        pieces = pieces + [jnp.zeros((below, part), jnp.float32)]
    return jnp.concatenate(pieces, 0)


def patched(block, spare, rows):
    place = lax.broadcasted_iota(jnp.int32, block.shape, 0)
    return jnp.where(first_core(), block, jnp.where(place < spare, block, rows))


def share_back(both_ref, out_ref):
    few = both_ref.shape[1] // 2
    used = out_ref.shape[2] // both_ref.shape[2]
    gram = both_ref[0, :few] + both_ref[1, :few]
    late = both_ref[1, few:]
    row = jnp.where(first_core(), flat(late, few - used, used), flat(gram, 0, used))
    for k in range(out_ref.shape[0]):
        out_ref[k] = row


def added(ref, start=0):
    total = ref[0, start:]
    for k in range(1, ref.shape[0]):
        total = total + ref[k, start:]
    return total


def bundle(crossed_ref, both_ref, early_ref, out_ref):
    half = crossed_ref.shape[1]
    coeffs = added(crossed_ref)
    out_ref[:, :half] = early_ref[...]
    for j in range(out_ref.shape[0]):
        piece = both_ref[1, (j + 1) * half : (j + 2) * half]
        out_ref[j, half:] = jnp.where(first_core(), piece, coeffs)


def join(got_ref, crossed_ref, traded_ref, out_ref):
    half = traded_ref.shape[2]
    late = jnp.where(first_core(), crossed_ref[...], traded_ref[0])
    rows = jnp.concatenate([got_ref[:, :half], late], 1)
    out_ref[...] = rows.reshape(out_ref.shape)


def remainder(got_ref, crossed_ref, traded_ref, st_ref, resid_ref, both_ref):
    modes, width, part = got_ref.shape
    count = st_ref.shape[0]
    half = width // 2
    lower = got_ref[:, :half]
    upper = jnp.where(first_core(), crossed_ref[...], traded_ref[0])
    rows = [block.reshape(modes * half, part) for block in (lower, upper)]
    coeffs = traded_ref[1].reshape(modes * half, 2 * count)
    back = dot3(coeffs.T, jnp.concatenate(rows, 1))
    resid = st_ref[...] - (back[:count, :part] + back[count:, part:])
    resid_ref[...] = resid
    few = both_ref.shape[0] // 2
    both_ref[:few] = pack_symmetric(dot3(resid, resid, 1, 1))
    both_ref[few:] = resid[count - few :]


def bundle_back(crossed_ref, rotated_ref, resid_ref, out_ref):
    modes, width, part = rotated_ref.shape
    count = resid_ref.shape[0]
    used = crossed_ref.shape[2] // part
    few = (used + 7) // 8 * 8
    gram = stacked(added(crossed_ref), part, few - used, 0)
    early = resid_ref[: count - few]
    late = patched(resid_ref[count - few :], few - used, gram)
    out_ref[:, :width] = rotated_ref[...]
    for j in range(modes):
        out_ref[j, width : width + count - few] = early
        out_ref[j, width + count - few :] = late


def last(crossed_ref, parts_ref, out_ref):
    modes = crossed_ref.shape[0]
    used = crossed_ref.shape[2] // parts_ref.shape[2]
    few = (used + 7) // 8 * 8
    out_ref[:modes] = crossed_ref[...]
    gram = added(parts_ref, parts_ref.shape[1] - few)
    out_ref[modes] = flat(gram, few - used, used)


def eliminate(gram):
    count = gram.shape[0]
    tiles = count // STEP
    shape = (STEP, 2 * count)
    lane = lax.broadcasted_iota(jnp.int32, shape, 1)
    sub = lax.broadcasted_iota(jnp.int32, shape, 0)
    wide = jnp.concatenate([gram, jnp.zeros((count, count), jnp.float32)], 1)
    rows = [
        jnp.where(lane == sub + (STEP * t + count), 1.0, wide[STEP * t : STEP * (t + 1)])
        for t in range(tiles)
    ]
    done = []
    for b in range(tiles):
        later = range(b + 1, tiles)
        first = STEP * b
        block = [
            jnp.broadcast_to(rows[b][:, first + k : first + k + 1], shape) for k in range(STEP)
        ]
        column = [
            {t: jnp.broadcast_to(rows[t][:, first + k : first + k + 1], shape) for t in later}
            for k in range(STEP)
        ]
        row = [jnp.broadcast_to(rows[b][k : k + 1], shape) for k in range(STEP)]
        pivot = {
            (i, k): jnp.broadcast_to(block[k][i : i + 1], shape)
            for i in range(STEP)
            for k in range(i + 1)
        }
        scaled = []
        for k in range(STEP):
            inverse = 1.0 / pivot[k, k]
            scaled.append(row[k] * inverse)
            for i in range(k + 1, STEP):
                ratio = pivot[i, k] * inverse
                for m in range(k + 1, i + 1):
                    pivot[i, m] = pivot[i, m] - ratio * pivot[m, k]
                row[i] = row[i] - ratio * row[k]
                for t in later:
                    column[i][t] = column[i][t] - ratio * column[k][t]
        for t in later:
            for k in range(STEP):
                rows[t] = rows[t] - column[k][t] * scaled[k]
        final = jnp.zeros(shape, jnp.float32)
        for k in range(STEP):
            final = jnp.where(sub == k, row[k] * lax.rsqrt(pivot[k, k]), final)
        done.append(jnp.where(lane >= sub + first, final, 0.0))
    return jnp.concatenate(done, 0)


def finish(scale, last_ref, lower_cols_ref, parts_ref, out_ref, factor_ref):
    count, width = lower_cols_ref.shape
    modes, _, part = parts_ref.shape
    used = last_ref.shape[3] // part
    few = (used + 7) // 8 * 8
    cut = width + count - few
    gram = stacked(last_ref[1, modes], part, 0, few - used)
    done = eliminate(unpack_symmetric(gram))
    factor_ref[...] = done[:, :count].T * (1.0 / scale)
    weights = dot3(lower_cols_ref[...].T, done[:, count:]) * scale
    for j in range(modes):
        late = stacked(last_ref[0, j], part, few - used, 0)
        late = patched(parts_ref[j, cut:], few - used, late)
        resid = jnp.concatenate([parts_ref[j, width:cut], late], 0)
        out_ref[:, j * part : (j + 1) * part] = parts_ref[j, :width] * scale + dot3(weights, resid)


def kernel(body, out, args, specs=None, scratch=(), params=LIMIT):
    return pl.pallas_call(
        body,
        out_shape=out,
        in_specs=specs or [VMEM] * len(args),
        out_specs=(VMEM,) * len(out) if isinstance(out, tuple) else VMEM,
        scratch_shapes=scratch,
        compiler_params=params,
    )(*args)


def over_space(block, depth):
    both = lax.all_gather(block, CORE, axis=0, tiled=False)
    few = block.shape[0] // 2
    return lax.all_to_all(
        kernel(share, struct(depth, few, block.shape[1]), (both,)), Z, 0, 0, tiled=True
    )


def cross(block, depth, modes):
    devices = np.arange(2 * depth * modes).reshape(depth, 2, modes)
    groups = devices[:, 1].T.tolist() + devices[:, 0].tolist()
    return lax.all_to_all(
        block, (Z, CORE) + MODE, 0, 0, tiled=True, axis_index_groups=groups
    )


def over_cores(block):
    return lax.all_gather(block, CORE, axis=0, tiled=False)


def over_mode(block):
    return lax.all_to_all(block, MODE, 0, 0, tiled=True)


def local(basis, snapshots, rotation):
    depth = lax.axis_size(Z)
    modes = lax.axis_size("y") * lax.axis_size("x")
    rows, width = basis.shape
    count = snapshots.shape[1]
    part = rows // modes
    half = width // 2
    few = 3 * count // 8
    used = count // 4 + 1
    total = rotation.shape[1]
    scale = float(rows * depth * 2) ** 0.5
    bt, st = basis.T, snapshots.T
    buffers = (
        pltpu.VMEM((width, rows), jnp.float32),
        pltpu.VMEM((count, rows), jnp.float32),
        pltpu.VMEM((count, 2 * width), jnp.float32),
        pltpu.SemaphoreType.DMA((2 * CHUNKS + 1,)),
    )
    first, early, st_own, lower_cols = kernel(
        project,
        (
            struct((modes + 1) * half, part),
            struct(modes, half, part),
            struct(count, part),
            struct(count, width),
        ),
        (bt, st, rotation),
        [HBM] * 3,
        buffers,
        FULL,
    )
    first = over_cores(first)
    crossed = kernel(share, struct(depth, half, part), (first,))
    crossed = cross(crossed, depth, modes)
    got = over_mode(kernel(bundle, struct(modes, width, part), (crossed, first, early)))
    traded = over_cores(got[:, half:])
    resid, both = kernel(
        remainder, (struct(count, part), struct(2 * few, part)), (got, crossed, traded, st_own)
    )
    own = kernel(join, struct(total, part), (got, crossed, traded))
    crossed = kernel(share_back, struct(depth, 1, used * part), (over_cores(both),))
    crossed = cross(crossed, depth, modes)
    rotated = dot(rotation[:total], own, 0, 0).reshape(modes, width, part)
    pieces = kernel(
        bundle_back, struct(modes, width + count, part), (crossed, rotated, resid)
    )
    parts = over_mode(pieces)
    gathered = over_cores(kernel(last, struct(modes + 1, 1, used * part), (crossed, parts)))
    out, factor = kernel(
        functools.partial(finish, scale),
        (struct(width, rows), struct(count, count)),
        (gathered, lower_cols, parts),
    )
    return out.T, factor


def solution(mesh):
    y, x = 4, 4
    split = Mesh(mesh.devices.reshape(-1, 2, y, x), ("z", "core", "y", "x"))
    space, mode = ("z", "core"), ("y", "x")
    placed = (P(space, mode), P(space, None), P())
    return jax.shard_map(
        local, mesh=split, in_specs=placed, out_specs=(P(space, mode), P()), check_vma=False
    )
```

```python
import functools

import jax
import jax.numpy as jnp
import numpy as np
from jax import lax
from jax.experimental import pallas as pl
from jax.experimental.pallas import tpu as pltpu
from jax.sharding import Mesh, PartitionSpec as P

HIGH = lax.Precision.HIGH
Z = "z"
CORE = "core"
MODE = ("y", "x")
STEP = 8
CHUNKS = 4
VMEM = pl.BlockSpec(memory_space=pltpu.VMEM)
HBM = pl.BlockSpec(memory_space=pltpu.HBM)
FULL = pltpu.CompilerParams(vmem_limit_bytes=55_700_000)
LIMIT = pltpu.CompilerParams(vmem_limit_bytes=32 << 20)


def struct(*shape):
    return jax.ShapeDtypeStruct(shape, jnp.float32)


def dot(a, b, left, right):
    return lax.dot_general(a, b, (((left,), (right,)), ((), ())), precision=HIGH)


def halves(a):
    top = a.astype(jnp.bfloat16)
    return top, (a - top.astype(jnp.float32)).astype(jnp.bfloat16)


def dot3(a, b, left=1, right=0):
    (ah, al), (bh, bl) = halves(a), halves(b)

    def one(p, q):
        dims = (((left,), (right,)), ((), ()))
        return lax.dot_general(p, q, dims, preferred_element_type=jnp.float32)

    return one(ah, bh) + (one(ah, bl) + one(al, bh))


def pack(block):
    half = block.shape[0] // 2
    return jnp.concatenate([block[:half], block[half:]], 1)


def square(size):
    return [lax.broadcasted_iota(jnp.int32, (size, size), d) for d in range(2)]


def pack_symmetric(block):
    half = block.shape[0] // 2
    step = half // 2
    row, col = square(half)
    last_quarter = block[half:, half:]
    mixed = jnp.where(row >= col, block[:half, :half], last_quarter)
    cross = block[half:, :half]
    diagonal = jnp.sum(jnp.where(row == col, last_quarter, 0.0), 0, keepdims=True)
    top = [mixed[:step], mixed[step:], cross[:step], cross[step:]]
    rest = [jnp.broadcast_to(diagonal, (8, half)), jnp.zeros((8, 3 * half), jnp.float32)]
    return jnp.concatenate([jnp.concatenate(top, 1), jnp.concatenate(rest, 1)], 0)


def unpack_symmetric(packed):
    half = packed.shape[1] // 4
    step = half // 2
    row, col = square(half)
    mixed, cross = (
        jnp.concatenate(
            [packed[:step, k * half : (k + 1) * half] for k in (first, first + 1)], 0
        )
        for first in (0, 2)
    )
    turned = mixed.T
    first = jnp.where(row >= col, mixed, turned)
    last_quarter = jnp.where(row < col, mixed, turned)
    diagonal = jnp.broadcast_to(packed[step : step + 1, :half], (half, half))
    last_quarter = jnp.where(row == col, diagonal, last_quarter)
    return jnp.concatenate(
        [jnp.concatenate([first, cross.T], 1), jnp.concatenate([cross, last_quarter], 1)], 0
    )


def project(
    bt_ref, st_ref, rot_ref, first_ref, early_ref, own_ref, cols_ref, b_buf, s_buf, r_buf, sems
):
    step = b_buf.shape[1] // CHUNKS
    place = lax.axis_index("y") * lax.axis_size("x") + lax.axis_index("x")
    count, width = cols_ref.shape
    wide = r_buf.shape[1]
    side = pl.ds(pl.multiple_of(place // (wide // width) * wide, wide), wide)
    columns = pltpu.make_async_copy(
        rot_ref.at[pl.ds(rot_ref.shape[0] - count, count), side], r_buf, sems.at[2 * CHUNKS]
    )
    columns.start()
    copies = []
    for i in range(CHUNKS):
        cut = pl.ds(i * step, step)
        for k, (src, dst) in enumerate(((bt_ref, b_buf), (st_ref, s_buf))):
            copy = pltpu.make_async_copy(src.at[:, cut], dst.at[:, cut], sems.at[2 * i + k])
            copy.start()
            copies.append(copy)
    _, half, part = early_ref.shape
    each = step // part
    total = None
    for i in range(CHUNKS):
        copies[2 * i].wait()
        copies[2 * i + 1].wait()
        cut = slice(i * step, (i + 1) * step)
        basis = b_buf[:, cut]
        term = dot3(basis, s_buf[:, cut], 1, 1)
        total = term if total is None else total + term
        for j in range(i * each, (i + 1) * each):
            piece = b_buf[:, j * part : (j + 1) * part]
            early_ref[j] = piece[:half]
            first_ref[(j + 1) * half : (j + 2) * half] = piece[half:]
    first_ref[:half] = pack(total)
    own_ref[...] = s_buf[:, pl.ds(pl.multiple_of(place * part, part), part)]
    columns.wait()
    found = r_buf[...]
    cols_ref[...] = jnp.where(place % 2 == 0, found[:, :width], found[:, width:])


def first_core():
    return lax.axis_index(CORE) == 0


def share(both_ref, out_ref):
    count, half, _ = out_ref.shape
    coeffs = both_ref[0, :half] + both_ref[1, :half]
    for k in range(count):
        piece = both_ref[1, (k + 1) * half : (k + 2) * half]
        out_ref[k] = jnp.where(first_core(), piece, coeffs)


def flat(block, first, used):
    return jnp.concatenate([block[r : r + 1] for r in range(first, first + used)], 1)


def stacked(row, part, above, below):
    pieces = [row[:, r : r + part] for r in range(0, row.shape[1], part)]
    if above:
        pieces = [jnp.zeros((above, part), jnp.float32)] + pieces
    if below:
        pieces = pieces + [jnp.zeros((below, part), jnp.float32)]
    return jnp.concatenate(pieces, 0)


def patched(block, spare, rows):
    place = lax.broadcasted_iota(jnp.int32, block.shape, 0)
    return jnp.where(first_core(), block, jnp.where(place < spare, block, rows))


def share_back(both_ref, out_ref):
    few = both_ref.shape[1] // 2
    used = out_ref.shape[2] // both_ref.shape[2]
    gram = both_ref[0, :few] + both_ref[1, :few]
    late = both_ref[1, few:]
    row = jnp.where(first_core(), flat(late, few - used, used), flat(gram, 0, used))
    for k in range(out_ref.shape[0]):
        out_ref[k] = row


def added(ref, start=0):
    total = ref[0, start:]
    for k in range(1, ref.shape[0]):
        total = total + ref[k, start:]
    return total


def bundle(crossed_ref, first_ref, early_ref, out_ref):
    half = crossed_ref.shape[1]
    coeffs = added(crossed_ref)
    out_ref[:, :half] = early_ref[...]
    for j in range(out_ref.shape[0]):
        piece = first_ref[(j + 1) * half : (j + 2) * half]
        out_ref[j, half:] = jnp.where(first_core(), piece, coeffs)


def trade(crossed_ref, got_ref, out_ref):
    half = crossed_ref.shape[1]
    out_ref[...] = jnp.where(first_core(), crossed_ref[...], got_ref[:, half:])


def join(got_ref, traded_ref, out_ref):
    half = traded_ref.shape[2]
    late = jnp.where(first_core(), got_ref[:, half:], traded_ref[0])
    rows = jnp.concatenate([got_ref[:, :half], late], 1)
    out_ref[...] = rows.reshape(out_ref.shape)


def remainder(got_ref, traded_ref, st_ref, resid_ref, both_ref):
    modes, width, part = got_ref.shape
    count = st_ref.shape[0]
    half = width // 2
    lower = got_ref[:, :half]
    upper = jnp.where(first_core(), got_ref[:, half:], traded_ref[0])
    rows = [block.reshape(modes * half, part) for block in (lower, upper)]
    coeffs = traded_ref[1].reshape(modes * half, 2 * count)
    back = dot3(coeffs.T, jnp.concatenate(rows, 1))
    resid = st_ref[...] - (back[:count, :part] + back[count:, part:])
    resid_ref[...] = resid
    few = both_ref.shape[0] // 2
    both_ref[:few] = pack_symmetric(dot3(resid, resid, 1, 1))
    both_ref[few:] = resid[count - few :]


def bundle_back(crossed_ref, rotated_ref, resid_ref, out_ref):
    modes, width, part = rotated_ref.shape
    count = resid_ref.shape[0]
    used = crossed_ref.shape[2] // part
    few = (used + 7) // 8 * 8
    gram = stacked(added(crossed_ref), part, few - used, 0)
    early = resid_ref[: count - few]
    late = patched(resid_ref[count - few :], few - used, gram)
    out_ref[:, :width] = rotated_ref[...]
    for j in range(modes):
        out_ref[j, width : width + count - few] = early
        out_ref[j, width + count - few :] = late


def last(crossed_ref, parts_ref, out_ref):
    modes = crossed_ref.shape[0]
    used = crossed_ref.shape[2] // parts_ref.shape[2]
    few = (used + 7) // 8 * 8
    out_ref[:modes] = crossed_ref[...]
    gram = added(parts_ref, parts_ref.shape[1] - few)
    out_ref[modes] = flat(gram, few - used, used)


def eliminate(gram):
    count = gram.shape[0]
    tiles = count // STEP
    shape = (STEP, 2 * count)
    lane = lax.broadcasted_iota(jnp.int32, shape, 1)
    sub = lax.broadcasted_iota(jnp.int32, shape, 0)
    wide = jnp.concatenate([gram, jnp.zeros((count, count), jnp.float32)], 1)
    rows = [
        jnp.where(lane == sub + (STEP * t + count), 1.0, wide[STEP * t : STEP * (t + 1)])
        for t in range(tiles)
    ]
    done = []
    for b in range(tiles):
        later = range(b + 1, tiles)
        first = STEP * b
        block = [
            jnp.broadcast_to(rows[b][:, first + k : first + k + 1], shape) for k in range(STEP)
        ]
        column = [
            {t: jnp.broadcast_to(rows[t][:, first + k : first + k + 1], shape) for t in later}
            for k in range(STEP)
        ]
        row = [jnp.broadcast_to(rows[b][k : k + 1], shape) for k in range(STEP)]
        pivot = {
            (i, k): jnp.broadcast_to(block[k][i : i + 1], shape)
            for i in range(STEP)
            for k in range(i + 1)
        }
        scaled = []
        for k in range(STEP):
            inverse = 1.0 / pivot[k, k]
            scaled.append(row[k] * inverse)
            for i in range(k + 1, STEP):
                ratio = pivot[i, k] * inverse
                for m in range(k + 1, i + 1):
                    pivot[i, m] = pivot[i, m] - ratio * pivot[m, k]
                row[i] = row[i] - ratio * row[k]
                for t in later:
                    column[i][t] = column[i][t] - ratio * column[k][t]
        for t in later:
            for k in range(STEP):
                rows[t] = rows[t] - column[k][t] * scaled[k]
        final = jnp.zeros(shape, jnp.float32)
        for k in range(STEP):
            final = jnp.where(sub == k, row[k] * lax.rsqrt(pivot[k, k]), final)
        done.append(jnp.where(lane >= sub + first, final, 0.0))
    return jnp.concatenate(done, 0)


def finish(scale, last_ref, lower_cols_ref, parts_ref, out_ref, factor_ref):
    count, width = lower_cols_ref.shape
    modes, _, part = parts_ref.shape
    used = last_ref.shape[3] // part
    few = (used + 7) // 8 * 8
    cut = width + count - few
    gram = stacked(last_ref[1, modes], part, 0, few - used)
    done = eliminate(unpack_symmetric(gram))
    factor_ref[...] = done[:, :count].T * (1.0 / scale)
    weights = dot3(lower_cols_ref[...].T, done[:, count:]) * scale
    for j in range(modes):
        late = stacked(last_ref[0, j], part, few - used, 0)
        late = patched(parts_ref[j, cut:], few - used, late)
        resid = jnp.concatenate([parts_ref[j, width:cut], late], 0)
        out_ref[:, j * part : (j + 1) * part] = parts_ref[j, :width] * scale + dot3(weights, resid)


def kernel(body, out, args, specs=None, scratch=(), params=LIMIT):
    return pl.pallas_call(
        body,
        out_shape=out,
        in_specs=specs or [VMEM] * len(args),
        out_specs=(VMEM,) * len(out) if isinstance(out, tuple) else VMEM,
        scratch_shapes=scratch,
        compiler_params=params,
    )(*args)


def over_space(block, depth):
    both = lax.all_gather(block, CORE, axis=0, tiled=False)
    few = block.shape[0] // 2
    return lax.all_to_all(
        kernel(share, struct(depth, few, block.shape[1]), (both,)), Z, 0, 0, tiled=True
    )


def cross(block, depth, modes):
    devices = np.arange(2 * depth * modes).reshape(depth, 2, modes)
    groups = devices[:, 1].T.tolist() + devices[:, 0].tolist()
    return lax.all_to_all(
        block, (Z, CORE) + MODE, 0, 0, tiled=True, axis_index_groups=groups
    )


def over_cores(block):
    return lax.all_gather(block, CORE, axis=0, tiled=False)


def over_mode(block):
    return lax.all_to_all(block, MODE, 0, 0, tiled=True)


def local(basis, snapshots, rotation):
    depth = lax.axis_size(Z)
    modes = lax.axis_size("y") * lax.axis_size("x")
    rows, width = basis.shape
    count = snapshots.shape[1]
    part = rows // modes
    half = width // 2
    few = 3 * count // 8
    used = count // 4 + 1
    total = rotation.shape[1]
    scale = float(rows * depth * 2) ** 0.5
    bt, st = basis.T, snapshots.T
    buffers = (
        pltpu.VMEM((width, rows), jnp.float32),
        pltpu.VMEM((count, rows), jnp.float32),
        pltpu.VMEM((count, 2 * width), jnp.float32),
        pltpu.SemaphoreType.DMA((2 * CHUNKS + 1,)),
    )
    first, early, st_own, lower_cols = kernel(
        project,
        (
            struct((modes + 1) * half, part),
            struct(modes, half, part),
            struct(count, part),
            struct(count, width),
        ),
        (bt, st, rotation),
        [HBM] * 3,
        buffers,
        FULL,
    )
    crossed = kernel(share, struct(depth, half, part), (over_cores(first),))
    crossed = cross(crossed, depth, modes)
    got = over_mode(kernel(bundle, struct(modes, width, part), (crossed, first, early)))
    traded = over_cores(kernel(trade, struct(modes, half, part), (crossed, got)))
    resid, both = kernel(
        remainder, (struct(count, part), struct(2 * few, part)), (got, traded, st_own)
    )
    crossed = kernel(share_back, struct(depth, 1, used * part), (over_cores(both),))
    crossed = cross(crossed, depth, modes)
    own = kernel(join, struct(total, part), (got, traded))
    rotated = dot(rotation[:total], own, 0, 0).reshape(modes, width, part)
    pieces = kernel(
        bundle_back, struct(modes, width + count, part), (crossed, rotated, resid)
    )
    parts = over_mode(pieces)
    gathered = over_cores(kernel(last, struct(modes + 1, 1, used * part), (crossed, parts)))
    out, factor = kernel(
        functools.partial(finish, scale),
        (struct(width, rows), struct(count, count)),
        (gathered, lower_cols, parts),
    )
    return out.T, factor


def solution(mesh):
    y, x = 4, 4
    split = Mesh(mesh.devices.reshape(-1, 2, y, x), ("z", "core", "y", "x"))
    space, mode = ("z", "core"), ("y", "x")
    placed = (P(space, mode), P(space, None), P())
    return jax.shard_map(
        local, mesh=split, in_specs=placed, out_specs=(P(space, mode), P()), check_vma=False
    )
```
